512 devices in a mesh: group: 8 (over z_hi, core), seq: 64 (over x, y, z_lo).
Axes of the slice: x: 4, y: 8, z: 8 (z_hi: 4, z_lo: 2; z = z_hi * 2 + z_lo), core: 2. Of those that a mesh axis runs over, the one named last changes fastest.
Arguments:
- latent_cache: bfloat16 [16, 16384, 576], P('group', 'seq'), may hold values from -6 to 6
- lengths: int32 [16], replicated, may hold values from 6553 to 16384, as said below
- moves: int32 [12, 4], replicated, may hold values from 0 to 7, as said below
- query_before: bfloat16 [16, 128, 576], P('group', 'seq'), may hold values from -256 to 256
- query_after: bfloat16 [32, 128, 576], P('group', 'seq'), may hold values from -256 to 256
Outputs:
- attended_before: bfloat16 [16, 128, 512], P('group', 'seq')
- lse_before: float32 [16, 128], P('group', 'seq')
- attended_after: bfloat16 [32, 128, 512], P('group', 'seq')
- lse_after: float32 [32, 128], P('group', 'seq')
- moved_cache: bfloat16 [16, 16384, 576], P('group', 'seq')
The draws below stay inside these ranges and needn't reach their ends.
Inputs may be any that keep to these rules, and one draw needn't show every extreme that they name: `lengths`: some request has exactly 16384 tokens and some exactly the least. Source group differs from destination group; no two moves share a source slot, a destination group and receiving slot, or a pair of source and destination groups; every group sends and receives at most 2 requests, and some group receives 2.
All inputs are finite; a program needn't handle non-finite values.
Results may differ from the reference program's by a relative error of at most 0.0054.
Values may be sent and summed in bfloat16 or wider, within the bound.
A program may use at most 64 MiB of HBM per device.

```python
import jax
import jax.numpy as jnp
from jax import lax

H = 128
LAT = 512
WIDTH = 576
REQ = 2
SPARE = 2
CAP = 16384
ROWS = 16
POST = 32
MOVED = 16
MOVES = 12
N_GROUP = 8


def move_table(key):
    key = jax.random.fold_in(key, 101)
    key_order, key_base, key_first, key_jump = jax.random.split(key, 4)
    order = jax.random.permutation(key_order, N_GROUP).astype(jnp.int32)
    base = jax.random.randint(key_base, (N_GROUP,), 0, REQ)
    first = jax.random.randint(key_first, (), 0, N_GROUP - 1)
    jump = jax.random.randint(key_jump, (), 0, max(N_GROUP - 2, 1))
    second = (first + 1 + jump) % (N_GROUP - 1)
    index = jnp.arange(MOVES, dtype=jnp.int32)
    rounds = index // N_GROUP
    place = index % N_GROUP
    shift = jnp.where(rounds == 0, first, second)
    source = order[place]
    target = order[(place + 1 + shift) % N_GROUP]
    slot = (base[source] + rounds) % REQ
    return jnp.stack([source, slot, target, rounds], axis=1).astype(jnp.int32)


def draw_latent_cache(key, part):
    key = jax.random.fold_in(key, 3)
    values = jnp.clip(jax.random.normal(key, (ROWS, CAP, WIDTH), jnp.float32), -6.0, 6.0)
    return values.astype(jnp.bfloat16)


def draw_lengths(key, part):
    key = jax.random.fold_in(key, 7)
    key_heavy, key_vals, key_pick = jax.random.split(key, 3)
    least = CAP * 2 // 5
    heavy = jax.random.randint(key_heavy, (N_GROUP, 1), 0, 3)
    values = jax.random.randint(key_vals, (N_GROUP, REQ), least, CAP + 1)
    values = least + (values - least) * (1 + heavy) // 3
    flat = values.reshape(ROWS)
    pick = jax.random.permutation(key_pick, ROWS)
    flat = flat.at[pick[0]].set(CAP).at[pick[1]].set(least)
    return flat.astype(jnp.int32)


def draw_moves(key, part):
    return move_table(key)


def draw_query_before(key, part):
    key = jax.random.fold_in(key, 5)
    values = jnp.clip(1.5 * jax.random.normal(key, (ROWS, H, WIDTH), jnp.float32), -9.0, 9.0)
    return values.astype(jnp.bfloat16)


def draw_query_after(key, part):
    key = jax.random.fold_in(key, 9)
    values = jnp.clip(1.5 * jax.random.normal(key, (POST, H, WIDTH), jnp.float32), -9.0, 9.0)
    return values.astype(jnp.bfloat16)


def setup_inputs(seed: int = 0) -> dict:
    streams_of = jax.random.split(jax.random.key(seed), 6)
    return {
        "latent_cache": draw_latent_cache(jax.random.fold_in(streams_of[5], 71), 0),
        "lengths": draw_lengths(jax.random.fold_in(streams_of[5], 71), 0),
        "moves": draw_moves(jax.random.fold_in(streams_of[5], 71), 0),
        "query_before": draw_query_before(jax.random.fold_in(streams_of[5], 71), 0),
        "query_after": draw_query_after(jax.random.fold_in(streams_of[5], 71), 0),
    }


SCALE = 192.0 ** -0.5


def attend(query, cache, length):
    scores = jnp.dot(query, cache.T, preferred_element_type=jnp.float32) * SCALE
    live = jnp.arange(cache.shape[0], dtype=jnp.int32) < length
    masked = jnp.where(live[None, :], scores, jnp.float32(-1e30))
    top = jnp.max(masked, axis=1)
    weights = jnp.where(live[None, :], jnp.exp(masked - top[:, None]), jnp.float32(0.0))
    total = jnp.sum(weights, axis=1)
    numer = jnp.dot(weights.astype(jnp.bfloat16), cache[:, :LAT], preferred_element_type=jnp.float32)
    empty = (length == 0).astype(jnp.float32)
    attended = (numer / (total + empty)[:, None]).astype(jnp.bfloat16)
    lse = jnp.where(length > 0, top + jnp.log(total + empty), jnp.float32(0.0))
    return attended, lse


def reference(latent_cache, lengths, moves, query_before, query_after):
    before_out, before_lse = lax.map(lambda item: attend(item[0], item[1], item[2]), (query_before, latent_cache, lengths))
    src_group = moves[:, 0]
    src_slot = moves[:, 1]
    dst_group = moves[:, 2]
    dst_spare = moves[:, 3]
    anchor = (src_group * REQ + src_slot).astype(jnp.int32)
    post = jnp.arange(POST, dtype=jnp.int32)
    group = post // (REQ + SPARE)
    within = post % (REQ + SPARE)
    resident = within < REQ
    home = (group * REQ + jnp.minimum(within, REQ - 1)).astype(jnp.int32)
    leaving = jnp.any((src_group[None, :] == group[:, None]) & (src_slot[None, :] == within[:, None]), axis=1) & resident
    landing = (dst_group[None, :] == group[:, None]) & (dst_spare[None, :] == (within - REQ)[:, None]) & (~resident)[:, None]
    arrived = jnp.any(landing, axis=1)
    incoming = jnp.sum(jnp.where(landing, anchor[None, :], 0), axis=1).astype(jnp.int32)
    source = jnp.where(resident, home, incoming).astype(jnp.int32)
    length_after = jnp.where((resident & ~leaving) | arrived, lengths[source], 0).astype(jnp.int32)
    after_out, after_lse = lax.map(lambda item: attend(item[0], latent_cache[item[1]], item[2]), (query_after, source, length_after))
    spare_index = jnp.arange(MOVED, dtype=jnp.int32)
    spare_group = spare_index // SPARE
    spare_slot = spare_index % SPARE
    filling = (dst_group[None, :] == spare_group[:, None]) & (dst_spare[None, :] == spare_slot[:, None])
    filled = jnp.any(filling, axis=1)
    taken = jnp.sum(jnp.where(filling, anchor[None, :], 0), axis=1).astype(jnp.int32)
    moved_cache = lax.map(lambda item: jnp.where(item[1], latent_cache[item[0]], jnp.zeros((CAP, WIDTH), jnp.bfloat16)), (taken, filled))
    return before_out, before_lse, after_out, after_lse, moved_cache
```

```python
import jax
import jax.numpy as jnp
from jax import lax
from jax.experimental import pallas as pl
from jax.experimental.pallas import tpu as pltpu
from jax.sharding import PartitionSpec as P

MESH = pl.DeviceIdType.MESH
LAT = 512
SCALE = 192.0 ** (-0.5)
LOW = -1e30
NX, NY, NZ, NG = 4, 8, 8, 8
F32, BF16 = jnp.float32, jnp.bfloat16


def loop(lo, hi, body):
    def step(i, carry):
        body(i)
        return carry

    lax.fori_loop(lo, hi, step, 0)


def to_column(row, n, offset):
    lane = lax.broadcasted_iota(jnp.int32, (n, 128), 1)
    sub = lax.broadcasted_iota(jnp.int32, (n, 128), 0)
    picked = jnp.where(lane == sub + offset, jnp.broadcast_to(row, (n, 128)), 0.0)
    return jnp.sum(picked, axis=1, keepdims=True)


def merge(parts, stats, n, offset):
    top = stats[0]
    for s in stats[1:]:
        top = jnp.maximum(top, s)
    weights = [jnp.exp(s - top) for s in stats]
    total = weights[0]
    for w in weights[1:]:
        total = total + w
    scale = 1.0 / total
    out = None
    for part, w in zip(parts, weights):
        term = to_column(w * scale, n, offset) * part.astype(F32)
        out = term if out is None else out + term
    return out, top + jnp.log(total)


def kernel(lens, moves, cache, qb, qa, ob, lb, oa, la, moved,
           cv, st, sel, rq, pb, pa, bs, g0, g1,
           s10, r10, t10, u10, s11, r11, t11, u11,
           s20, r20, t20, u20, s21, r21, t21, u21,
           s3, r3, b3, t3, u3,
           lsem, p1s, p1r, p2s, p2r, zs, zr, as_, ar, xs, xr, ms, mr, ns, nr, os_, or_):
    req, shard, width = cv.shape
    piece = shard // NG
    g, s = lax.axis_index("group"), lax.axis_index("seq")
    zh, core = g // 2, g % 2
    x, y, zl = s // (2 * NY), (s // 2) % NY, s % 2
    v = (zh * 2 + zl) * 2 + core

    def ring(w):
        z, c = w // 2, w % 2
        return {"group": (z // 2) * 2 + c, "seq": (x * NY + y) * 2 + z % 2}

    def at_group(h):
        return {"group": h, "seq": s}

    def at_x(i):
        return {"group": g, "seq": (i * NY + y) * 2 + zl}

    def at_y(i):
        return {"group": g, "seq": (x * NY + i) * 2 + zl}

    vp = ((zh * 2 + (1 - zl)) * 2) + core

    def remote(src, dst, ss, rs, dev):
        return pltpu.make_async_remote_copy(
            src_ref=src, dst_ref=dst, send_sem=ss, recv_sem=rs, device_id=dev, device_id_type=MESH
        )

    load = pltpu.make_async_copy(cache, cv, lsem.at[0])
    load.start()
    barrier = pltpu.get_barrier_semaphore()

    def greet(dev):
        pl.semaphore_signal(barrier, inc=1, device_id=dev, device_id_type=MESH)

    loop(1, 16, lambda d: greet(ring((v + d) % 16)))
    loop(1, NY, lambda d: greet(at_y((y + d) % NY)))
    loop(1, NX, lambda d: greet(at_x((x + d) % NX)))

    zero = jnp.zeros((1, 128), F32)
    for i in range(NX):
        t10[i], u10[i], t21[i], u21[i] = zero, zero, zero, zero
    for i in range(NY):
        t11[i], u11[i], t20[i], u20[i] = zero, zero, zero, zero
    for r in range(req):
        t3[r] = zero
    rq[v] = qa[req:]
    table = [[moves[i, c] for c in range(4)] for i in range(moves.shape[0])]

    def look(match):
        a = b = c = jnp.int32(0)
        for m in table:
            hit = match(m)
            a = a + jnp.where(hit, m[0] * req + m[1], 0)
            b = b + jnp.where(hit, m[2] * req + m[3], 0)
            c = c + jnp.where(hit, 1, 0)
        return a, b, c > 0

    out_to = [look(lambda m, r=r: (m[0] == g) & (m[1] == r)) for r in range(req)]
    came = [look(lambda m, k=k: (m[2] == g) & (m[3] == k)) for k in range(req)]
    load.wait()
    pl.semaphore_wait(barrier, 15 + NY - 1 + NX - 1)

    def z1(d):
        return remote(qa.at[pl.ds(req, req)], rq.at[v], zs.at[d], zr.at[d], ring((v + d) % 16))

    zq = remote(qb, pb, zs.at[0], zr.at[0], ring(vp))
    zp = remote(qa.at[pl.ds(0, req)], pa, zs.at[16], zr.at[16], ring(vp))
    zq.start()
    zp.start()
    loop(1, 16, lambda d: z1(d).start())

    def p1(d):
        h = (g + d) % NG
        return remote(cv.at[:, pl.ds(h * piece, piece), :], st.at[g], p1s.at[d], p1r.at[d], at_group(h))

    loop(1, NG, lambda d: p1(d).start())
    keep = pltpu.make_async_copy(cv.at[:, pl.ds(g * piece, piece), :], st.at[g], lsem.at[1])
    keep.start()

    zq.wait()
    zp.wait()
    loop(1, 16, lambda d: z1(d).wait())
    for r in range(req):
        _, target, leaves = out_to[r]
        for i in range(2):
            mine = zl == i
            before = jnp.where(mine, qb[r].astype(F32), pb[r].astype(F32))
            stay = jnp.where(mine, qa[r].astype(F32), pa[r].astype(F32))
            tg = target // req
            away = rq[((tg // 2) * 2 + i) * 2 + tg % 2, target % req].astype(F32)
            bs[r, 4 * i : 4 * i + 2] = before
            bs[r, 4 * i + 2 : 4 * i + 4] = jnp.where(leaves, away, stay)
    g0[x, y] = bs[0].astype(BF16)
    g1[y, x] = bs[1].astype(BF16)

    def a0(d):
        return remote(g0.at[x, y], g0.at[x, y], as_.at[d], ar.at[d], at_y((y + d) % NY))

    def a1(d):
        return remote(g1.at[y, x], g1.at[y, x], as_.at[NY + d], ar.at[NY + d], at_x((x + d) % NX))

    def b0(d):
        return remote(g0.at[x], g0.at[x], xs.at[d], xr.at[d], at_x((x + d) % NX))

    def b1(d):
        return remote(g1.at[y], g1.at[y], xs.at[NX + d], xr.at[NX + d], at_y((y + d) % NY))

    loop(1, NX, lambda d: a1(d).start())
    loop(1, NY, lambda d: a0(d).start())
    loop(1, NX, lambda d: a1(d).wait())
    loop(1, NY, lambda d: b1(d).start())
    loop(1, NY, lambda d: a0(d).wait())
    loop(1, NX, lambda d: b0(d).start())

    position = s * shard + lax.broadcasted_iota(jnp.int32, (shard, 1), 0)
    length = [lens[g * req + r] for r in range(req)]

    def attend(q, r):
        n = q.shape[0]
        scores = lax.dot_general(
            cv[r], q, (((1,), (1,)), ((), ())), preferred_element_type=F32
        ) * SCALE
        live = jnp.broadcast_to(position, (shard, n)) < length[r]
        masked = jnp.where(live, scores, LOW)
        top = jnp.max(masked, axis=0, keepdims=True)
        weights = jnp.where(live, jnp.exp(masked - top), 0.0)
        total = jnp.sum(weights, axis=0, keepdims=True)
        some = total > 0.0
        safe = jnp.where(some, total, 1.0)
        part = lax.dot_general(
            (weights * (1.0 / safe)).astype(BF16), cv[r, :, :LAT],
            (((0,), (0,)), ((), ())), preferred_element_type=F32,
        )
        return part.astype(BF16), jnp.where(some, top + jnp.log(safe), LOW)

    def rows(block):
        a, b, w = block.shape
        return block.astype(F32).reshape(a * b, w).astype(BF16)

    n0, n1 = NY * 8, NX * 8

    def c0(d):
        to = (x + d) % NX
        return (remote(s10.at[to], r10.at[x], ms.at[0, d], mr.at[0, d], at_x(to)),
                remote(t10.at[to], u10.at[x], ms.at[1, d], mr.at[1, d], at_x(to)))

    def c1(d):
        to = (y + d) % NY
        return (remote(s11.at[to], r11.at[y], ms.at[2, d], mr.at[2, d], at_y(to)),
                remote(t11.at[to], u11.at[y], ms.at[3, d], mr.at[3, d], at_y(to)))

    def each(copies, what):
        for c in copies:
            getattr(c, what)()

    part, lse = attend(rows(g1[y]), 1)
    r11[y] = part
    u11[y, :, 0:n1] = lse
    part, lse = attend(rows(g0[x]), 0)
    r10[x] = part
    u10[x, :, 0:n0] = lse

    keep.wait()
    loop(1, NG, lambda d: p1(d).wait())

    def pick(i):
        d, k = i // req, i % req
        a, _, found = look(lambda m: (m[2] == d) & (m[3] == k))
        value = st[a // req, a % req]
        sel[d, k] = jnp.where(found, value, jnp.zeros_like(value))

    loop(0, NG * req, pick)

    def p2(d):
        h = (g + d) % NG
        return remote(sel.at[h], moved.at[:, pl.ds(g * piece, piece), :], p2s.at[d], p2r.at[d], at_group(h))

    loop(1, NG, lambda d: p2(d).start())
    own = pltpu.make_async_copy(sel.at[g], moved.at[:, pl.ds(g * piece, piece), :], lsem.at[2])
    own.start()

    def block1(d):
        b1(d).wait_recv()
        frm = (y + NY - d) % NY
        part, lse = attend(rows(g1[frm]), 1)
        s11[frm] = part
        t11[frm, :, 0:n1] = lse
        each(c1(NY - d), "start")

    def block0(d):
        b0(d).wait_recv()
        frm = (x + NX - d) % NX
        part, lse = attend(rows(g0[frm]), 0)
        s10[frm] = part
        t10[frm, :, 0:n0] = lse
        each(c0(NX - d), "start")

    loop(1, NX, block0)
    loop(1, NY, block1)

    loop(1, NX, lambda d: b0(d).wait_send())
    loop(1, NY, lambda d: b1(d).wait_send())

    def e0(d):
        to = (y + d) % NY
        return (remote(s20.at[to], r20.at[y], ns.at[0, d], nr.at[0, d], at_y(to)),
                remote(t20.at[0], u20.at[y], ns.at[1, d], nr.at[1, d], at_y(to)))

    def e1(d):
        to = (x + d) % NX
        return (remote(s21.at[to], r21.at[x], ns.at[2, d], nr.at[2, d], at_x(to)),
                remote(t21.at[0], u21.at[x], ns.at[3, d], nr.at[3, d], at_x(to)))

    loop(1, NX, lambda d: each(c0(d), "wait"))
    part, lse = merge([r10[i] for i in range(NX)], [u10[i] for i in range(NX)], n0, 0)
    s20[...] = part.reshape(NY, 8, LAT).astype(BF16)
    t20[0] = lse
    r20[y] = s20[y]
    u20[y] = lse
    loop(1, NY, lambda d: each(e0(d), "start"))

    loop(1, NY, lambda d: each(c1(d), "wait"))
    part, lse = merge([r11[i] for i in range(NY)], [u11[i] for i in range(NY)], n1, 0)
    s21[...] = part.reshape(NX, 8, LAT).astype(BF16)
    t21[0] = lse
    r21[x] = s21[x]
    u21[x] = lse
    loop(1, NX, lambda d: each(e1(d), "start"))

    loop(1, NX, lambda d: each(e1(d), "wait"))
    part1, lse1 = merge([r21[i] for i in range(NX)], [u21[i] for i in range(NX)], 8, 8 * x)
    loop(1, NY, lambda d: each(e0(d), "wait"))
    part0, lse0 = merge([r20[i] for i in range(NY)], [u20[i] for i in range(NY)], 8, 8 * y)
    t3[0] = pltpu.roll(jnp.broadcast_to(lse0, (8, 128)), (128 - 8 * y) % 128, 1)[0:1]
    t3[1] = pltpu.roll(jnp.broadcast_to(lse1, (8, 128)), (128 - 8 * x) % 128, 1)[0:1]
    for r, part in enumerate((part0, part1)):
        for i in range(2):
            for b in range(2):
                s3[i, b, r] = part[4 * i + 2 * b : 4 * i + 2 * b + 2]

    def f(d):
        w = (v + d) % 16
        return (remote(s3.at[(w // 2) % 2, 1], r3.at[v], os_.at[0, d], or_.at[0, d], ring(w)),
                remote(t3, u3.at[v], os_.at[1, d], or_.at[1, d], ring(w)))

    fb = remote(s3.at[1 - zl, 0], b3, os_.at[0, 0], or_.at[0, 0], ring(vp))
    fb.start()
    loop(1, 16, lambda d: each(f(d), "start"))
    r3[v] = s3[zl, 1]
    u3[v] = t3[...]
    fb.wait()
    loop(1, 16, lambda d: each(f(d), "wait"))

    def turned(row):
        return pltpu.roll(jnp.broadcast_to(row, (8, 128)), (128 - 4 * zl) % 128, 1)[0:1]

    def shifted(row):
        return pltpu.roll(jnp.broadcast_to(row, (8, 128)), 126, 1)[0:1]

    for r in range(req):
        stats = [turned(u3[v, r]), turned(u3[vp, r])]
        alive = length[r] > 0
        out, lse = merge([s3[zl, 0, r], b3[r]], stats, 2, 0)
        ob[r] = jnp.where(alive, out, 0.0).astype(BF16)
        lb[r : r + 1, :] = jnp.where(alive, lse, 0.0)[:, 0:2]
        stays = alive & jnp.logical_not(out_to[r][2])
        out, lse = merge([r3[v, r], r3[vp, r]], stats, 2, 2)
        oa[r] = jnp.where(stays, out, 0.0).astype(BF16)
        la[r : r + 1, :] = shifted(jnp.where(stays, lse, 0.0))[:, 0:2]
    for k in range(req):
        a, _, found = came[k]
        sg, sl = a // req, a % req
        w = [((sg // 2) * 2 + i) * 2 + sg % 2 for i in range(2)]
        stats = [turned(u3[j, sl]) for j in w]
        alive = found & (lens[a] > 0)
        out, lse = merge([r3[j, sl] for j in w], stats, 2, 2)
        oa[req + k] = jnp.where(alive, out, 0.0).astype(BF16)
        la[req + k : req + k + 1, :] = shifted(jnp.where(alive, lse, 0.0))[:, 0:2]

    own.wait()
    loop(1, NG, lambda d: p2(d).wait())


def local(cache, lengths, moves, qb, qa):
    req, shard, width = cache.shape
    heads = qb.shape[1]
    piece = shard // NG
    n0, n1 = NY * 8, NX * 8
    vm, dma = pltpu.VMEM, pltpu.SemaphoreType.DMA
    spec = pl.BlockSpec(memory_space=pltpu.VMEM)
    smem = pl.BlockSpec(memory_space=pltpu.SMEM)
    anywhere = pl.BlockSpec(memory_space=pl.ANY)
    shape = jax.ShapeDtypeStruct
    return pl.pallas_call(
        kernel,
        out_shape=(
            shape((req, heads, LAT), BF16),
            shape((req, heads), F32),
            shape((2 * req, heads, LAT), BF16),
            shape((2 * req, heads), F32),
            shape((req, shard, width), BF16),
        ),
        in_specs=[smem, smem, anywhere, spec, spec],
        out_specs=(spec, spec, spec, spec, anywhere),
        scratch_shapes=[
            vm((req, shard, width), BF16),
            vm((NG, req, piece, width), BF16),
            vm((NG, req, piece, width), BF16),
            vm((16, req, heads, width), BF16),
            vm((req, heads, width), BF16),
            vm((req, heads, width), BF16),
            vm((req, 8, width), F32),
            vm((NX, NY, 8, width), BF16),
            vm((NY, NX, 8, width), BF16),
            vm((NX, n0, LAT), BF16), vm((NX, n0, LAT), BF16), vm((NX, 1, 128), F32), vm((NX, 1, 128), F32),
            vm((NY, n1, LAT), BF16), vm((NY, n1, LAT), BF16), vm((NY, 1, 128), F32), vm((NY, 1, 128), F32),
            vm((NY, 8, LAT), BF16), vm((NY, 8, LAT), BF16), vm((NY, 1, 128), F32), vm((NY, 1, 128), F32),
            vm((NX, 8, LAT), BF16), vm((NX, 8, LAT), BF16), vm((NX, 1, 128), F32), vm((NX, 1, 128), F32),
            vm((2, 2, req, heads, LAT), F32),
            vm((16, req, heads, LAT), F32),
            vm((req, heads, LAT), F32),
            vm((req, 1, 128), F32),
            vm((16, req, 1, 128), F32),
            dma((3,)),
            dma((NG,)), dma((NG,)), dma((NG,)), dma((NG,)),
            dma((17,)), dma((17,)),
            dma((NY + NX,)), dma((NY + NX,)),
            dma((NX + NY,)), dma((NX + NY,)),
            dma((4, NY)), dma((4, NY)),
            dma((4, NY)), dma((4, NY)),
            dma((2, 16)), dma((2, 16)),
        ],
        name="decode_and_move",
        compiler_params=pltpu.CompilerParams(
            collective_id=0, has_side_effects=True, vmem_limit_bytes=32 << 20
        ),
    )(lengths, moves, cache, qb, qa)


def solution(mesh):
    placed = (P("group", "seq", None), P(), P(), P("group", "seq", None), P("group", "seq", None))
    return jax.shard_map(
        local,
        mesh=mesh,
        in_specs=placed,
        out_specs=(
            P("group", "seq", None),
            P("group", "seq"),
            P("group", "seq", None),
            P("group", "seq"),
            P("group", "seq", None),
        ),
        check_vma=False,
    )
```

```python
import jax
import jax.numpy as jnp
from jax import lax
from jax.experimental import pallas as pl
from jax.experimental.pallas import tpu as pltpu
from jax.sharding import PartitionSpec as P

MESH = pl.DeviceIdType.MESH
LAT = 512
SCALE = 192.0 ** (-0.5)
LOW = -1e30
NX, NY, NZ, NG = 4, 8, 8, 8
F32, BF16 = jnp.float32, jnp.bfloat16


def loop(lo, hi, body):
    for i in range(lo, hi):
        body(i)


def div(a, b):
    return lax.div(a, jnp.int32(b))


def rem(a, b):
    return lax.rem(a, jnp.int32(b))


def to_column(row, n):
    lane = lax.broadcasted_iota(jnp.int32, (n, 128), 1)
    sub = lax.broadcasted_iota(jnp.int32, (n, 128), 0)
    picked = jnp.where(lane == sub, jnp.broadcast_to(row, (n, 128)), 0.0)
    return jnp.sum(picked, axis=1, keepdims=True)


def to_row(column):
    n = column.shape[0]
    lane = lax.broadcasted_iota(jnp.int32, (n, 128), 1)
    sub = lax.broadcasted_iota(jnp.int32, (n, 128), 0)
    spread = jnp.where(lane == sub, jnp.broadcast_to(column, (n, 128)), 0.0)
    return jnp.sum(spread, axis=0, keepdims=True)


def weigh(stats):
    top = stats[0]
    for s in stats[1:]:
        top = jnp.maximum(top, s)
    weights = [jnp.exp(s - top) for s in stats]
    total = weights[0]
    for w in weights[1:]:
        total = total + w
    scale = 1.0 / total
    return [w * scale for w in weights], top + jnp.log(total)


def blend(parts, columns):
    out = None
    for part, w in zip(parts, columns):
        term = w * part.astype(F32)
        out = term if out is None else out + term
    return out


def tail(column):
    n = column.shape[0]
    high = column.astype(BF16).astype(F32)
    rest = column - high
    mid = rest.astype(BF16).astype(F32)
    lane = lax.broadcasted_iota(jnp.int32, (n, 128), 1)
    terms = jnp.where(lane == 0, high, jnp.where(lane == 1, mid, jnp.where(lane == 2, rest - mid, 0.0)))
    return terms.astype(BF16)


def untail(block):
    return jnp.sum(block.astype(F32), axis=1, keepdims=True)


def join(blocks):
    weights, lse = weigh([untail(b[:, LAT:]) for b in blocks])
    return blend([b[:, :LAT] for b in blocks], weights), lse


def kernel(lens_h, moves_h, cache, qb_h, qa_h, ob, lb, oa, la, moved,
           lens, moves, qb, qa, cv, st0, st1, sel0, sel1, rq, pb, pa, bs, gq,
           s1, r1, t1, u1, s2, r2, s3, r3, b3,
           lsem, p1s, p1r, p2s, p2r, zs, zr, as_, ar, xs, xr, ms, mr, ns, nr, os_, or_):
    req, width, shard = cv.shape
    high = width // (NG // 2)
    st, sel = (st0, st1), (sel0, sel1)
    cuts = ((0, st0.shape[2]), (st0.shape[2], st1.shape[2]))
    g, s = lax.axis_index("group"), lax.axis_index("seq")
    zh, core = div(g, 2), rem(g, 2)
    x, y, zl = div(s, 2 * NY), rem(div(s, 2), NY), rem(s, 2)
    v = (zh * 2 + zl) * 2 + core

    def ring(w):
        z, c = div(w, 2), rem(w, 2)
        return {"group": div(z, 2) * 2 + c, "seq": (x * NY + y) * 2 + rem(z, 2)}

    def at_group(h):
        return {"group": h, "seq": s}

    def at_x(i):
        return {"group": g, "seq": (i * NY + y) * 2 + zl}

    def at_y(i):
        return {"group": g, "seq": (x * NY + i) * 2 + zl}

    vp = ((zh * 2 + (1 - zl)) * 2) + core
    far_x, far_y, far_z = (2, 1, 3), (4, 3, 5, 2, 6, 1, 7), (8, 9, 7, 6, 10, 5, 11, 4, 12, 3, 13, 2, 14, 1, 15)
    near_x = (1, 3, 2)

    def piece(ref, h, c):
        low, size = cuts[c]
        at = pl.multiple_of(div(h, 2) * high + low, 16)
        return ref.at[:, pl.ds(at, size), pl.ds(pl.multiple_of(rem(h, 2) * 128, 128), 128)]

    def remote(src, dst, ss, rs, dev):
        return pltpu.make_async_remote_copy(
            src_ref=src, dst_ref=dst, send_sem=ss, recv_sem=rs, device_id=dev, device_id_type=MESH
        )

    barrier = pltpu.get_barrier_semaphore()

    def greet(dev):
        pl.semaphore_signal(barrier, inc=1, device_id=dev, device_id_type=MESH)

    for d in far_z:
        greet(ring(rem(v + d, 16)))
    for d in far_y:
        greet(at_y(rem(y + d, NY)))
    for d in far_x:
        greet(at_x(rem(x + d, NX)))
    loads = [
        pltpu.make_async_copy(a, b, lsem.at[i])
        for i, (a, b) in enumerate(((qb_h, qb), (qa_h, qa), (cache, cv), (moves_h, moves), (lens_h, lens)))
    ]
    for copy in loads:
        copy.start()
    for copy in loads:
        copy.wait()
    pl.semaphore_wait(barrier, 15 + NY - 1 + NX - 1)

    def z1(d):
        return remote(qa.at[pl.ds(req, req)], rq.at[v], zs.at[d], zr.at[d], ring(rem(v + d, 16)))

    zq = remote(qb, pb, zs.at[0], zr.at[0], ring(vp))
    zp = remote(qa.at[pl.ds(0, req)], pa, zs.at[16], zr.at[16], ring(vp))
    zq.start()
    for d in far_z:
        z1(d).start()
    zp.start()

    def p1(d, c):
        h = rem(g + d, NG)
        return remote(piece(cv, h, c), st[c].at[g], p1s.at[c, d], p1r.at[c, d], at_group(h))

    for c in range(2):
        loop(1, NG, lambda d: p1(d, c).start())
    keep = [pltpu.make_async_copy(piece(cv, g, c), st[c].at[g], lsem.at[5 + c]) for c in range(2)]
    for copy in keep:
        copy.start()

    rq[v] = qa[req:]
    table = [[moves[c, i] for c in range(4)] for i in range(moves.shape[1])]

    def look(match):
        a = b = c = jnp.int32(0)
        for m in table:
            hit = match(m)
            a = a + jnp.where(hit, m[0] * req + m[1], 0)
            b = b + jnp.where(hit, m[2] * req + m[3], 0)
            c = c + jnp.where(hit, 1, 0)
        return a, b, c > 0

    out_to = [look(lambda m, r=r: (m[0] == g) & (m[1] == r)) for r in range(req)]
    came = [look(lambda m, k=k: (m[2] == g) & (m[3] == k)) for k in range(req)]
    length = [lens[g * req + r] for r in range(req)]

    def ga(u, d):
        return remote(gq.at[u, x, y], gq.at[u, x, y], as_.at[u, d], ar.at[u, d], at_y(rem(y + d, NY)))

    def gb(u, d):
        return remote(gq.at[u, x], gq.at[u, x], xs.at[u, d], xr.at[u, d], at_x(rem(x + d, NX)))

    zq.wait()
    for r in range(req):
        for i in range(2):
            mine = zl == i
            bs[0, 4 * i + 2 * r : 4 * i + 2 * r + 2] = jnp.where(mine, qb[r].astype(F32), pb[r].astype(F32))
    gq[0, x, y] = bs[0].astype(BF16)
    for d in far_y:
        ga(0, d).start()

    zp.wait()
    for d in far_z:
        z1(d).wait()
    for r in range(req):
        _, target, leaves = out_to[r]
        tg = div(target, req)
        for i in range(2):
            stay = jnp.where(zl == i, qa[r].astype(F32), pa[r].astype(F32))
            away = rq[(div(tg, 2) * 2 + i) * 2 + rem(tg, 2), rem(target, req)].astype(F32)
            bs[1, 4 * i + 2 * r : 4 * i + 2 * r + 2] = jnp.where(leaves, away, stay)
    gq[1, x, y] = bs[1].astype(BF16)
    for d in far_y:
        ga(1, d).start()

    n = NY * 8
    row = lax.broadcasted_iota(jnp.int32, (n, 1), 0)
    second = rem(div(row, 2), 2) == 1
    position = s * shard + lax.broadcasted_iota(jnp.int32, (n, shard), 1)

    def attend(u, i):
        q = gq[u, i].astype(F32).reshape(n, width).astype(BF16)
        scores = jnp.where(
            second,
            jnp.dot(q, cv[1], preferred_element_type=F32),
            jnp.dot(q, cv[0], preferred_element_type=F32),
        ) * SCALE
        live = position < jnp.where(second, length[1], length[0])
        masked = jnp.where(live, scores, LOW)
        top = jnp.max(masked, axis=1, keepdims=True)
        weights = jnp.where(live, jnp.exp(masked - top), 0.0)
        total = jnp.sum(weights, axis=1, keepdims=True)
        some = total > 0.0
        safe = jnp.where(some, total, 1.0)
        weights = weights * (1.0 / safe)
        part = None
        for r in range(req):
            mine = jnp.where(second == (r == 1), weights, 0.0).astype(BF16)
            term = lax.dot_general(
                mine, cv[r, :LAT, :], (((1,), (1,)), ((), ())), preferred_element_type=F32
            )
            part = term if part is None else part + term
        return part.astype(BF16), to_row(jnp.where(some, top + jnp.log(safe), LOW))

    def rc(u, d):
        to = rem(x + d, NX)
        return (remote(s1.at[u, to], r1.at[u, x], ms.at[u, 0, d], mr.at[u, 0, d], at_x(to)),
                remote(t1.at[u, to], u1.at[u, x], ms.at[u, 1, d], mr.at[u, 1, d], at_x(to)))

    def each(copies, what):
        for c in copies:
            getattr(c, what)()

    def own_block(u):
        r1[u, x], u1[u, x] = attend(u, x)

    def other_block(u, d):
        gb(u, d).wait_recv()
        frm = rem(x + NX - d, NX)
        s1[u, frm], t1[u, frm] = attend(u, frm)
        each(rc(u, NX - d), "start")

    def forward(c):
        keep[c].wait()
        loop(1, NG, lambda d: p1(d, c).wait())

        def pick(i, carry):
            d, k = div(i, req), rem(i, req)
            a, _, found = look(lambda m: (m[2] == d) & (m[3] == k))
            value = st[c][div(a, req), rem(a, req)]
            sel[c][d, k] = jnp.where(found, value, jnp.zeros_like(value))
            return carry

        lax.fori_loop(0, NG * req, pick, 0)
        loop(1, NG, lambda d: p2(d, c).start())
        own[c].start()

    def p2(d, c):
        h = rem(g + d, NG)
        return remote(sel[c].at[h], piece(moved, g, c), p2s.at[c, d], p2r.at[c, d], at_group(h))

    own = [pltpu.make_async_copy(sel[c].at[g], piece(moved, g, c), lsem.at[7 + c]) for c in range(2)]

    for d in far_y:
        ga(0, d).wait()
    for d in far_x:
        gb(0, d).start()
    own_block(0)
    for d in far_y:
        ga(1, d).wait()
    for d in far_x:
        gb(1, d).start()
    own_block(1)
    forward(0)
    for d in near_x:
        other_block(0, d)
    forward(1)
    for d in near_x:
        other_block(1, d)

    def re(u, d):
        to = rem(y + d, NY)
        return remote(s2.at[u, to], r2.at[u, y], ns.at[u, d], nr.at[u, d], at_y(to))

    def second_step(u):
        for d in near_x:
            gb(u, d).wait_send()
            each(rc(u, d), "wait")
        weights, lse = weigh([u1[u, i] for i in range(NX)])
        part = blend([r1[u, i] for i in range(NX)], [to_column(w, n) for w in weights])
        s2[u, :, :, :LAT] = part.reshape(NY, 8, LAT).astype(BF16)
        s2[u, :, :, LAT:] = tail(to_column(lse, n)).astype(F32).reshape(NY, 8, 128).astype(BF16)
        r2[u, y] = s2[u, y]
        for d in far_y:
            re(u, d).start()

    def third_step(u):
        for d in far_y:
            re(u, d).wait()
        part, lse = join([r2[u, i] for i in range(NY)])
        end = tail(lse)
        for i in range(2):
            for r in range(req):
                rows = slice(4 * i + 2 * r, 4 * i + 2 * r + 2)
                s3[u, i, r, :, :LAT] = part[rows].astype(BF16)
                s3[u, i, r, :, LAT:] = end[rows]

    second_step(0)
    second_step(1)

    def rf(d):
        w = rem(v + d, 16)
        return remote(s3.at[1, rem(div(w, 2), 2)], r3.at[v], os_.at[d], or_.at[d], ring(w))

    fb = remote(s3.at[0, 1 - zl], b3, os_.at[0], or_.at[0], ring(vp))
    third_step(0)
    fb.start()
    third_step(1)
    for d in far_z:
        rf(d).start()
    r3[v] = s3[1, zl]
    fb.wait()
    for r in range(req):
        out, lse = join([s3[0, zl, r], b3[r]])
        alive = length[r] > 0
        ob[r] = jnp.where(alive, out, 0.0).astype(BF16)
        lb[r : r + 1, :] = to_row(jnp.where(alive, lse, 0.0))[:, 0:2]
    for d in far_z:
        rf(d).wait()
    for r in range(req):
        out, lse = join([r3[v, r], r3[vp, r]])
        stays = (length[r] > 0) & jnp.logical_not(out_to[r][2])
        oa[r] = jnp.where(stays, out, 0.0).astype(BF16)
        la[:, r : r + 1] = jnp.where(stays, lse, 0.0)
    for k in range(req):
        a, _, found = came[k]
        sg, sl = div(a, req), rem(a, req)
        out, lse = join([r3[(div(sg, 2) * 2 + i) * 2 + rem(sg, 2), sl] for i in range(2)])
        alive = found & (lens[a] > 0)
        oa[req + k] = jnp.where(alive, out, 0.0).astype(BF16)
        la[:, req + k : req + k + 1] = jnp.where(alive, lse, 0.0)

    for c in range(2):
        own[c].wait()
        loop(1, NG, lambda d: p2(d, c).wait())


def place(*refs):
    n = len(refs) // 3
    sems = refs[-1]
    parts = []
    for i, (a, c, b) in enumerate(zip(refs[:n], refs[n : 2 * n], refs[2 * n : 3 * n])):
        parts.append((pltpu.make_async_copy(a, b, sems.at[0, i]), pltpu.make_async_copy(b, c, sems.at[1, i])))
    for a, _ in parts:
        a.start()
    for a, b in parts:
        a.wait()
        b.start()
    for _, b in parts:
        b.wait()


def local(cache, lengths, moves, qb, qa):
    req, shard, width = cache.shape
    heads = qb.shape[1]
    high = width // (NG // 2)
    first = high // 32 * 16 + 16
    n = NY * 8
    wide = LAT + 128
    vm, dma = pltpu.VMEM, pltpu.SemaphoreType.DMA
    spec = pl.BlockSpec(memory_space=pltpu.VMEM)
    hbm = pl.BlockSpec(memory_space=pltpu.HBM)
    anywhere = pl.BlockSpec(memory_space=pl.ANY)
    shape = jax.ShapeDtypeStruct
    outs = (
        shape((req, heads, LAT), BF16),
        shape((req, heads), F32),
        shape((2 * req, heads, LAT), BF16),
        shape((heads, 2 * req), F32),
        shape((req, width, shard), BF16),
    )
    got = pl.pallas_call(
        kernel,
        out_shape=outs,
        in_specs=[hbm] * 5,
        out_specs=(spec, spec, spec, spec, anywhere),
        scratch_shapes=[
            pltpu.SMEM(lengths.shape, jnp.int32),
            pltpu.SMEM(moves.shape[::-1], jnp.int32),
            vm(qb.shape, BF16),
            vm(qa.shape, BF16),
            vm((req, width, shard), BF16),
            vm((NG, req, first, 128), BF16), vm((NG, req, high - first, 128), BF16),
            vm((NG, req, first, 128), BF16), vm((NG, req, high - first, 128), BF16),
            vm((16, req, heads, width), BF16),
            vm((req, heads, width), BF16),
            vm((req, heads, width), BF16),
            vm((2, 8, width), F32),
            vm((2, NX, NY, 8, width), BF16),
            vm((2, NX, n, LAT), BF16), vm((2, NX, n, LAT), BF16),
            vm((2, NX, 1, 128), F32), vm((2, NX, 1, 128), F32),
            vm((2, NY, 8, wide), BF16), vm((2, NY, 8, wide), BF16),
            vm((2, 2, req, heads, wide), BF16),
            vm((16, req, heads, wide), BF16),
            vm((req, heads, wide), BF16),
            dma((9,)),
            dma((2, NG)), dma((2, NG)), dma((2, NG)), dma((2, NG)),
            dma((17,)), dma((17,)),
            dma((2, NY)), dma((2, NY)),
            dma((2, NX)), dma((2, NX)),
            dma((2, 2, NX)), dma((2, 2, NX)),
            dma((2, NY)), dma((2, NY)),
            dma((16,)), dma((16,)),
        ],
        name="decode_and_move",
        compiler_params=pltpu.CompilerParams(
            collective_id=0, has_side_effects=True, vmem_limit_bytes=63 << 20
        ),
    )(lengths, moves.T, jnp.transpose(cache, (0, 2, 1)), qb, qa)
    ob, lb, oa, la, moved = pl.pallas_call(
        place,
        out_shape=outs,
        in_specs=[hbm] * 5,
        out_specs=(hbm,) * 5,
        scratch_shapes=[*(vm(o.shape, o.dtype) for o in outs), dma((2, 5))],
        name="place",
        compiler_params=pltpu.CompilerParams(vmem_limit_bytes=63 << 20),
    )(*got)
    return ob, lb, oa, la.T, jnp.transpose(moved, (0, 2, 1))


def solution(mesh):
    placed = (P("group", "seq", None), P(), P(), P("group", "seq", None), P("group", "seq", None))
    return jax.shard_map(
        local,
        mesh=mesh,
        in_specs=placed,
        out_specs=(
            P("group", "seq", None),
            P("group", "seq"),
            P("group", "seq", None),
            P("group", "seq"),
            P("group", "seq", None),
        ),
        check_vma=False,
    )
```

```python
import jax
import jax.numpy as jnp
from jax import lax
from jax.experimental import pallas as pl
from jax.experimental.pallas import tpu as pltpu
from jax.sharding import PartitionSpec as P

MESH = pl.DeviceIdType.MESH
LAT = 512
SCALE = 192.0 ** (-0.5)
LOW = -1e30
CUTS = (48, 48, 48)
NX, NY, NZ, NG = 4, 8, 8, 8
F32, BF16 = jnp.float32, jnp.bfloat16


def loop(lo, hi, body):
    for i in range(lo, hi):
        body(i)


def div(a, b):
    return lax.div(a, jnp.int32(b))


def rem(a, b):
    return lax.rem(a, jnp.int32(b))


def to_column(row, n):
    lane = lax.broadcasted_iota(jnp.int32, (n, 128), 1)
    sub = lax.broadcasted_iota(jnp.int32, (n, 128), 0)
    picked = jnp.where(lane == sub, jnp.broadcast_to(row, (n, 128)), 0.0)
    return jnp.sum(picked, axis=1, keepdims=True)


def to_row(column):
    n = column.shape[0]
    lane = lax.broadcasted_iota(jnp.int32, (n, 128), 1)
    sub = lax.broadcasted_iota(jnp.int32, (n, 128), 0)
    spread = jnp.where(lane == sub, jnp.broadcast_to(column, (n, 128)), 0.0)
    return jnp.sum(spread, axis=0, keepdims=True)


def weigh(stats):
    top = stats[0]
    for s in stats[1:]:
        top = jnp.maximum(top, s)
    weights = [jnp.exp(s - top) for s in stats]
    total = weights[0]
    for w in weights[1:]:
        total = total + w
    scale = 1.0 / total
    return [w * scale for w in weights], top + jnp.log(total)


def blend(parts, columns):
    out = None
    for part, w in zip(parts, columns):
        term = w * part.astype(F32)
        out = term if out is None else out + term
    return out


def tail(column):
    n = column.shape[0]
    high = column.astype(BF16).astype(F32)
    rest = column - high
    mid = rest.astype(BF16).astype(F32)
    lane = lax.broadcasted_iota(jnp.int32, (n, 128), 1)
    terms = jnp.where(lane == 0, high, jnp.where(lane == 1, mid, jnp.where(lane == 2, rest - mid, 0.0)))
    return terms.astype(BF16)


def untail(block):
    return jnp.sum(block.astype(F32), axis=1, keepdims=True)


def join(blocks):
    weights, lse = weigh([untail(b[:, LAT:]) for b in blocks])
    return blend([b[:, :LAT] for b in blocks], weights), lse


def look(table, match):
    a = b = c = jnp.int32(0)
    for m in table:
        hit = match(m)
        a = a + jnp.where(hit, m[0] * 2 + m[1], 0)
        b = b + jnp.where(hit, m[2] * 2 + m[3], 0)
        c = c + jnp.where(hit, 1, 0)
    return a, b, c > 0


def read_table(moves):
    return [[moves[c, i] for c in range(4)] for i in range(moves.shape[1])]


def kernel(lens_h, moves_h, cache, qb_h, qa_h, kept, b3, r3, moved,
           lens, moves, qb, qa, cv, st, sel, rq, qx, pb, pa, bs, gq,
           s1, r1, t1, u1, s2, r2, s3, s4,
           lsem, p1s, p1r, p2s, p2r, zs, zr, as_, ar, xs, xr, ms, mr, ns, nr, os_, or_):
    req, width, shard = cv.shape
    high = width // (NG // 2)
    cuts, low = [], 0
    for ref in st:
        cuts.append((low, ref.shape[2]))
        low += ref.shape[2]
    n_cuts = len(cuts)
    g, s = lax.axis_index("group"), lax.axis_index("seq")
    zh, core = div(g, 2), rem(g, 2)
    x, y, zl = div(s, 2 * NY), rem(div(s, 2), NY), rem(s, 2)
    v = (zh * 2 + zl) * 2 + core

    def ring(w):
        z, c = div(w, 2), rem(w, 2)
        return {"group": div(z, 2) * 2 + c, "seq": (x * NY + y) * 2 + rem(z, 2)}

    def at_group(h):
        return {"group": h, "seq": s}

    def at_x(i):
        return {"group": g, "seq": (i * NY + y) * 2 + zl}

    def at_y(i):
        return {"group": g, "seq": (x * NY + i) * 2 + zl}

    vp = ((zh * 2 + (1 - zl)) * 2) + core
    far_x, far_y, far_z = (2, 1, 3), (4, 3, 5, 2, 6, 1, 7), (8, 9, 7, 6, 10, 5, 11, 4, 12, 3, 13, 2, 14, 1, 15)
    near_x = (1, 3, 2)

    def piece(ref, h, c):
        low, size = cuts[c]
        at = pl.multiple_of(div(h, 2) * high + low, 16)
        return ref.at[:, pl.ds(at, size), pl.ds(pl.multiple_of(rem(h, 2) * 128, 128), 128)]

    def remote(src, dst, ss, rs, dev):
        return pltpu.make_async_remote_copy(
            src_ref=src, dst_ref=dst, send_sem=ss, recv_sem=rs, device_id=dev, device_id_type=MESH
        )

    def arrived(ref, sem):
        remote(ref, ref, sem, sem, ring(vp)).wait_recv()

    def left(ref, sem):
        remote(ref, ref, sem, sem, ring(vp)).wait_send()

    barrier = pltpu.get_barrier_semaphore()

    def greet(dev):
        pl.semaphore_signal(barrier, inc=1, device_id=dev, device_id_type=MESH)

    for d in far_z:
        greet(ring(rem(v + d, 16)))
    for d in far_y:
        greet(at_y(rem(y + d, NY)))
    for d in far_x:
        greet(at_x(rem(x + d, NX)))
    loads = [
        pltpu.make_async_copy(a, b, lsem.at[i])
        for i, (a, b) in enumerate(((qb_h, qb), (qa_h, qa), (cache, cv), (moves_h, moves), (lens_h, lens)))
    ]
    for copy in loads:
        copy.start()
    for copy in loads:
        copy.wait()
    table = read_table(moves)
    out_to = [look(table, lambda m, r=r: (m[0] == g) & (m[1] == r)) for r in range(req)]
    came = [look(table, lambda m, k=k: (m[2] == g) & (m[3] == k)) for k in range(req)]
    length = [lens[g * req + r] for r in range(req)]

    a, _, found = came[1]
    for h in range(NG):
        last = found & (div(a, req) == h)
        qx[h] = jnp.where(last, qa[req + 1].astype(F32), qa[req].astype(F32)).astype(BF16)
    rq[v] = qx[0]
    pl.semaphore_wait(barrier, 15 + NY - 1 + NX - 1)

    def z1(d):
        to = ring(rem(v + d, 16))
        return remote(qx.at[to["group"]], rq.at[v], zs.at[2], zr.at[2], to)

    zq = remote(qb, pb, zs.at[0], zr.at[0], ring(vp))
    zp = remote(qa.at[pl.ds(0, req)], pa, zs.at[1], zr.at[1], ring(vp))
    zq.start()
    for d in far_z:
        z1(d).start()
    zp.start()

    def p1(d, c):
        h = rem(g + d, NG)
        return remote(piece(cv, h, c), st[c].at[g], p1s.at[c], p1r.at[c], at_group(h))

    for c in range(n_cuts):
        loop(1, NG, lambda d: p1(d, c).start())
    keep = [pltpu.make_async_copy(piece(cv, g, c), st[c].at[g], lsem.at[7 + c]) for c in range(n_cuts)]
    for copy in keep:
        copy.start()

    rings = ((1, 7), (2, 6), (3, 5, 4))

    def ga(u, d):
        band = min(d, NY - d, 3) - 1
        return remote(gq.at[u, x, y], gq.at[u, x, y], as_.at[u], ar.at[u, band], at_y(rem(y + d, NY)))

    def spread(u):
        for d in far_y:
            ga(u, d).start()
        relay(u, (0,))

    def relay(u, steps):
        for e in steps:
            block = gq.at[u, x, rem(y + e, NY)]
            for d in far_x:
                remote(block, block, xs.at[u], xr.at[u, d], at_x(rem(x + d, NX))).start()

    def pass_on(u, band):
        arrived(gq.at[u, x, pl.ds(0, len(rings[band]))], ar.at[u, band])
        relay(u, rings[band])

    zq.wait()
    for r in range(req):
        for i in range(2):
            mine = zl == i
            bs[0, 4 * i + 2 * r : 4 * i + 2 * r + 2] = jnp.where(mine, qb[r].astype(F32), pb[r].astype(F32))
    gq[0, x, y] = bs[0].astype(BF16)
    spread(0)
    pass_on(0, 0)
    pass_on(0, 1)

    zp.wait()
    arrived(rq.at[pl.ds(0, 15)], zr.at[2])
    for r in range(req):
        _, target, leaves = out_to[r]
        tg = div(target, req)
        for i in range(2):
            stay = jnp.where(zl == i, qa[r].astype(F32), pa[r].astype(F32))
            away = rq[(div(tg, 2) * 2 + i) * 2 + rem(tg, 2)].astype(F32)
            bs[1, 4 * i + 2 * r : 4 * i + 2 * r + 2] = jnp.where(leaves, away, stay)
    gq[1, x, y] = bs[1].astype(BF16)
    spread(1)

    n = NY * 8
    row = lax.broadcasted_iota(jnp.int32, (n, 1), 0)
    second = rem(div(row, 2), 2) == 1
    position = s * shard + lax.broadcasted_iota(jnp.int32, (n, shard), 1)

    def attend(u, i):
        q = gq[u, i].astype(F32).reshape(n, width).astype(BF16)
        scores = jnp.where(
            second,
            jnp.dot(q, cv[1], preferred_element_type=F32),
            jnp.dot(q, cv[0], preferred_element_type=F32),
        ) * SCALE
        live = position < jnp.where(second, length[1], length[0])
        masked = jnp.where(live, scores, LOW)
        top = jnp.max(masked, axis=1, keepdims=True)
        weights = jnp.where(live, jnp.exp(masked - top), 0.0)
        total = jnp.sum(weights, axis=1, keepdims=True)
        some = total > 0.0
        safe = jnp.where(some, total, 1.0)
        weights = weights * (1.0 / safe)
        part = None
        for r in range(req):
            mine = jnp.where(second == (r == 1), weights, 0.0).astype(BF16)
            term = lax.dot_general(
                mine, cv[r, :LAT, :], (((1,), (1,)), ((), ())), preferred_element_type=F32
            )
            part = term if part is None else part + term
        return part.astype(BF16), to_row(jnp.where(some, top + jnp.log(safe), LOW))

    def rc(u, d):
        to = rem(x + d, NX)
        return (remote(s1.at[u, to], r1.at[u, x], ms.at[u, 0], mr.at[u, 0], at_x(to)),
                remote(t1.at[u, to], u1.at[u, x], ms.at[u, 1], mr.at[u, 1], at_x(to)))

    def each(copies, what):
        for c in copies:
            getattr(c, what)()

    def own_block(u):
        r1[u, x], u1[u, x] = attend(u, x)

    def other_block(u, d):
        frm = rem(x + NX - d, NX)
        arrived(gq.at[u, frm], xr.at[u, d])
        s1[u, frm], t1[u, frm] = attend(u, frm)
        each(rc(u, NX - d), "start")

    def forward(c):
        keep[c].wait()
        arrived(st[c].at[pl.ds(0, NG - 1)], p1r.at[c])

        def pick(i, carry):
            d, k = div(i, req), rem(i, req)
            a, _, found = look(table, lambda m: (m[2] == d) & (m[3] == k))
            value = st[c][div(a, req), rem(a, req)]
            sel[c][d, k] = jnp.where(found, value, jnp.zeros_like(value))
            return carry

        lax.fori_loop(0, NG * req, pick, 0)
        loop(1, NG, lambda d: p2(d, c).start())
        own[c].start()

    def p2(d, c):
        h = rem(g + d, NG)
        return remote(sel[c].at[h], piece(moved, g, c), p2s.at[c], p2r.at[c], at_group(h))

    own = [pltpu.make_async_copy(sel[c].at[g], piece(moved, g, c), lsem.at[7 + n_cuts + c]) for c in range(n_cuts)]

    def re(u, d):
        to = rem(y + d, NY)
        return remote(s2.at[u, to], r2.at[u, y], ns.at[u], nr.at[u], at_y(to))

    def second_step(u):
        arrived(r1.at[u, pl.ds(0, NX - 1)], mr.at[u, 0])
        arrived(u1.at[u, pl.ds(0, NX - 1)], mr.at[u, 1])
        weights, lse = weigh([u1[u, i] for i in range(NX)])
        part = blend([r1[u, i] for i in range(NX)], [to_column(w, n) for w in weights])
        s2[u, :, :, :LAT] = part.reshape(NY, 8, LAT).astype(BF16)
        s2[u, :, :, LAT:] = tail(to_column(lse, n)).astype(F32).reshape(NY, 8, 128).astype(BF16)
        r2[u, y] = s2[u, y]
        for d in far_y:
            re(u, d).start()

    def third_step(u):
        arrived(r2.at[u, pl.ds(0, NY - 1)], nr.at[u])
        part, lse = join([r2[u, i] for i in range(NY)])
        end = tail(lse)
        for i in range(2):
            for r in range(req):
                rows = slice(4 * i + 2 * r, 4 * i + 2 * r + 2)
                s3[u, i, r, :, :LAT] = part[rows].astype(BF16)
                s3[u, i, r, :, LAT:] = end[rows]

    pass_on(0, 2)
    own_block(0)
    for band in range(3):
        pass_on(1, band)
    own_block(1)
    forward(0)
    for d in near_x:
        other_block(0, d)
    forward(1)
    for d in near_x:
        other_block(1, d)
    second_step(0)
    forward(2)
    second_step(1)

    def rf(d):
        w = rem(v + d, 16)
        to = ring(w)
        return remote(s4.at[rem(div(w, 2), 2), to["group"]], r3.at[v], os_.at[2], or_.at[2], to)

    fb = remote(s3.at[0, 1 - zl], b3.at[0], os_.at[0], or_.at[0], ring(vp))
    fa = remote(s3.at[1, 1 - zl], b3.at[1], os_.at[1], or_.at[1], ring(vp))
    stays = [pltpu.make_async_copy(s3.at[u, zl], kept.at[u], lsem.at[5]) for u in range(2)]
    fill = pltpu.make_async_copy(s3.at[1, zl, 0], r3.at[v], lsem.at[6])
    third_step(1)
    _, target, leaves = out_to[1]
    for i in range(2):
        for h in range(NG):
            last = leaves & (div(target, req) == h)
            s4[i, h] = jnp.where(last, s3[1, i, 1], s3[1, i, 0])
    for d in far_z:
        rf(d).start()
    fa.start()
    fill.start()
    third_step(0)
    fb.start()
    for copy in stays:
        copy.start()
    fb.wait()
    fa.wait()
    fill.wait()
    pltpu.make_async_copy(kept, kept, lsem.at[5]).wait()
    arrived(r3.at[pl.ds(0, 15)], or_.at[2])
    for c in range(n_cuts):
        own[c].wait()
        arrived(sel[c].at[pl.ds(0, NG - 1)], p2r.at[c])

    left(rq.at[pl.ds(0, 15)], zs.at[2])
    left(r3.at[pl.ds(0, 15)], os_.at[2])
    for u in range(2):
        left(gq.at[u, x, pl.ds(0, NY - 1)], as_.at[u])
        left(gq.at[u, pl.ds(0, NX - 1)], xs.at[u])
        left(s1.at[u, pl.ds(0, NX - 1)], ms.at[u, 0])
        left(t1.at[u, pl.ds(0, NX - 1)], ms.at[u, 1])
        left(s2.at[u, pl.ds(0, NY - 1)], ns.at[u])
    for c in range(n_cuts):
        left(st[c].at[pl.ds(0, NG - 1)], p1s.at[c])
        left(sel[c].at[pl.ds(0, NG - 1)], p2s.at[c])


def finish(lens_h, moves_h, mine_h, b3_h, r3_h, moved, ob_h, lb_h, oa_h, la_h, moved_to,
           lens, moves, mine, b3, r3, ob, lb, oa, la, hold, sems):
    req = ob.shape[0]
    g, zl = lax.axis_index("group"), rem(lax.axis_index("seq"), 2)
    takes = [pltpu.make_async_copy(moved.at[r], hold.at[r], sems.at[0, r]) for r in range(req)]
    puts = [pltpu.make_async_copy(hold.at[r], moved_to.at[r], sems.at[1, r]) for r in range(req)]
    loads = [
        pltpu.make_async_copy(a, b, sems.at[0, req + i])
        for i, (a, b) in enumerate(((lens_h, lens), (moves_h, moves), (mine_h, mine), (b3_h, b3), (r3_h, r3)))
    ]
    stores = [
        pltpu.make_async_copy(a, b, sems.at[1, req + i])
        for i, (a, b) in enumerate(((ob, ob_h), (lb, lb_h), (oa, oa_h), (la, la_h)))
    ]
    for copy in takes + loads:
        copy.start()
    for copy in loads:
        copy.wait()
    table = read_table(moves)
    for r in range(req):
        alive = lens[g * req + r] > 0
        out, lse = join([mine[0, r], b3[0, r]])
        ob[r] = jnp.where(alive, out, 0.0).astype(BF16)
        lb[r : r + 1, :] = to_row(jnp.where(alive, lse, 0.0))[:, 0:2]
        _, _, leaves = look(table, lambda m, r=r: (m[0] == g) & (m[1] == r))
        stays = alive & jnp.logical_not(leaves)
        out, lse = join([mine[1, r], b3[1, r]])
        oa[r] = jnp.where(stays, out, 0.0).astype(BF16)
        la[:, r : r + 1] = jnp.where(stays, lse, 0.0)
    for copy, put in zip(takes, puts):
        copy.wait()
        put.start()
    for k in range(req):
        a, _, found = look(table, lambda m, k=k: (m[2] == g) & (m[3] == k))
        sg = div(a, req)
        out, lse = join([r3[(div(sg, 2) * 2 + i) * 2 + rem(sg, 2)] for i in range(2)])
        alive = found & (lens[a] > 0)
        oa[req + k] = jnp.where(alive, out, 0.0).astype(BF16)
        la[:, req + k : req + k + 1] = jnp.where(alive, lse, 0.0)
    for copy in stores:
        copy.start()
    for copy in stores + puts:
        copy.wait()


def local(cache, lengths, moves, qb, qa):
    req, shard, width = cache.shape
    heads = qb.shape[1]
    n = NY * 8
    wide = LAT + 128
    vm, dma = pltpu.VMEM, pltpu.SemaphoreType.DMA
    hbm = pl.BlockSpec(memory_space=pltpu.HBM)
    shape = jax.ShapeDtypeStruct
    outs = (
        shape((req, heads, LAT), BF16),
        shape((req, heads), F32),
        shape((2 * req, heads, LAT), BF16),
        shape((heads, 2 * req), F32),
        shape((req, width, shard), BF16),
    )
    sent = (
        shape((2, req, heads, wide), BF16),
        shape((2, req, heads, wide), BF16),
        shape((16, heads, wide), BF16),
        outs[4],
    )
    moves = moves.T
    got = pl.pallas_call(
        kernel,
        out_shape=sent,
        in_specs=[hbm] * 5,
        out_specs=(hbm,) * 4,
        scratch_shapes=[
            pltpu.SMEM(lengths.shape, jnp.int32),
            pltpu.SMEM(moves.shape, jnp.int32),
            vm(qb.shape, BF16),
            vm(qa.shape, BF16),
            vm((req, width, shard), BF16),
            *[tuple(vm((NG, req, size, 128), BF16) for size in CUTS)] * 2,
            vm((16, heads, width), BF16),
            vm((NG, heads, width), BF16),
            vm((req, heads, width), BF16),
            vm((req, heads, width), BF16),
            vm((2, 8, width), F32),
            vm((2, NX, NY, 8, width), BF16),
            vm((2, NX, n, LAT), BF16), vm((2, NX, n, LAT), BF16),
            vm((2, NX, 1, 128), F32), vm((2, NX, 1, 128), F32),
            vm((2, NY, 8, wide), BF16), vm((2, NY, 8, wide), BF16),
            vm((2, 2, req, heads, wide), BF16),
            vm((2, NG, heads, wide), BF16),
            dma((7 + 2 * len(CUTS),)),
            *[dma((len(CUTS),))] * 4,
            dma((3,)), dma((3,)),
            dma((2,)), dma((2, 3)),
            dma((2,)), dma((2, NX)),
            dma((2, 2)), dma((2, 2)),
            dma((2,)), dma((2,)),
            dma((3,)), dma((3,)),
        ],
        name="decode_and_move",
        compiler_params=pltpu.CompilerParams(
            collective_id=0, has_side_effects=True, vmem_limit_bytes=63 << 20
        ),
    )(lengths, moves, jnp.transpose(cache, (0, 2, 1)), qb, qa)
    ob, lb, oa, la, moved = pl.pallas_call(
        finish,
        out_shape=outs,
        in_specs=[hbm] * 6,
        out_specs=(hbm,) * 5,
        scratch_shapes=[
            pltpu.SMEM(lengths.shape, jnp.int32),
            pltpu.SMEM(moves.shape, jnp.int32),
            *(vm(o.shape, o.dtype) for o in sent[:3]),
            *(vm(o.shape, o.dtype) for o in outs),
            dma((2, req + 5)),
        ],
        name="finish",
        compiler_params=pltpu.CompilerParams(vmem_limit_bytes=63 << 20),
    )(lengths, moves, *got)
    return ob, lb, oa, la.T, jnp.transpose(moved, (0, 2, 1))


def solution(mesh):
    placed = (P("group", "seq", None), P(), P(), P("group", "seq", None), P("group", "seq", None))
    return jax.shard_map(
        local,
        mesh=mesh,
        in_specs=placed,
        out_specs=(
            P("group", "seq", None),
            P("group", "seq"),
            P("group", "seq", None),
            P("group", "seq"),
            P("group", "seq", None),
        ),
        check_vma=False,
    )
```

```python
import jax
import jax.numpy as jnp
from jax import lax
from jax.experimental import pallas as pl
from jax.experimental.pallas import tpu as pltpu
from jax.sharding import PartitionSpec as P

MESH = pl.DeviceIdType.MESH
LAT = 512
SCALE = 192.0 ** (-0.5)
LOW = -1e30
CUTS = (48, 48, 48)
NX, NY, NZ, NG = 4, 8, 8, 8
F32, BF16 = jnp.float32, jnp.bfloat16


def loop(lo, hi, body):
    for i in range(lo, hi):
        body(i)


def div(a, b):
    return lax.div(a, jnp.int32(b))


def rem(a, b):
    return lax.rem(a, jnp.int32(b))


def to_column(row, n):
    lane = lax.broadcasted_iota(jnp.int32, (n, 128), 1)
    sub = lax.broadcasted_iota(jnp.int32, (n, 128), 0)
    picked = jnp.where(lane == sub, jnp.broadcast_to(row, (n, 128)), 0.0)
    return jnp.sum(picked, axis=1, keepdims=True)


def to_row(column):
    n = column.shape[0]
    lane = lax.broadcasted_iota(jnp.int32, (n, 128), 1)
    sub = lax.broadcasted_iota(jnp.int32, (n, 128), 0)
    spread = jnp.where(lane == sub, jnp.broadcast_to(column, (n, 128)), 0.0)
    return jnp.sum(spread, axis=0, keepdims=True)


def weigh(stats):
    top = stats[0]
    for s in stats[1:]:
        top = jnp.maximum(top, s)
    weights = [jnp.exp(s - top) for s in stats]
    total = weights[0]
    for w in weights[1:]:
        total = total + w
    scale = 1.0 / total
    return [w * scale for w in weights], top + jnp.log(total)


def blend(parts, columns):
    out = None
    for part, w in zip(parts, columns):
        term = w * part.astype(F32)
        out = term if out is None else out + term
    return out


def tail(column):
    n = column.shape[0]
    high = column.astype(BF16).astype(F32)
    rest = column - high
    mid = rest.astype(BF16).astype(F32)
    lane = lax.broadcasted_iota(jnp.int32, (n, 128), 1)
    terms = jnp.where(lane == 0, high, jnp.where(lane == 1, mid, jnp.where(lane == 2, rest - mid, 0.0)))
    return terms.astype(BF16)


def untail(block):
    return jnp.sum(block.astype(F32), axis=1, keepdims=True)


def join(blocks):
    weights, lse = weigh([untail(b[:, LAT:]) for b in blocks])
    return blend([b[:, :LAT] for b in blocks], weights), lse


def look(table, match):
    a = b = c = jnp.int32(0)
    for m in table:
        hit = match(m)
        a = a + jnp.where(hit, m[0] * 2 + m[1], 0)
        b = b + jnp.where(hit, m[2] * 2 + m[3], 0)
        c = c + jnp.where(hit, 1, 0)
    return a, b, c > 0


def read_table(moves):
    return [[moves[c, i] for c in range(4)] for i in range(moves.shape[1])]


def kernel(lens_h, moves_h, cache, qb_h, qa_h, kept, b3, r3, moved,
           lens, moves, qb, qa, cv, st, sel, rq, qx, pb, pa, bs, gq,
           s1, r1, t1, u1, s2, r2, s3, s4,
           lsem, p1s, p1r, p2s, p2r, zs, zr, as_, ar, xs, xr, ms, mr, ns, nr, os_, or_):
    req, width, shard = cv.shape
    high = width // (NG // 2)
    cuts, low = [], 0
    for ref in st:
        cuts.append((low, ref.shape[2]))
        low += ref.shape[2]
    n_cuts = len(cuts)
    g, s = lax.axis_index("group"), lax.axis_index("seq")
    zh, core = div(g, 2), rem(g, 2)
    x, y, zl = div(s, 2 * NY), rem(div(s, 2), NY), rem(s, 2)
    v = (zh * 2 + zl) * 2 + core

    def ring(w):
        z, c = div(w, 2), rem(w, 2)
        return {"group": div(z, 2) * 2 + c, "seq": (x * NY + y) * 2 + rem(z, 2)}

    def at_group(h):
        return {"group": h, "seq": s}

    def at_x(i):
        return {"group": g, "seq": (i * NY + y) * 2 + zl}

    def at_y(i):
        return {"group": g, "seq": (x * NY + i) * 2 + zl}

    vp = ((zh * 2 + (1 - zl)) * 2) + core
    far_x, far_y, far_z = (2, 1, 3), (4, 3, 5, 2, 6, 1, 7), (8, 9, 7, 6, 10, 5, 11, 4, 12, 3, 13, 2, 14, 1, 15)
    near_x = (1, 3, 2)

    def piece(ref, h, c):
        low, size = cuts[c]
        at = pl.multiple_of(div(h, 2) * high + low, 16)
        return ref.at[:, pl.ds(at, size), pl.ds(pl.multiple_of(rem(h, 2) * 128, 128), 128)]

    def remote(src, dst, ss, rs, dev):
        return pltpu.make_async_remote_copy(
            src_ref=src, dst_ref=dst, send_sem=ss, recv_sem=rs, device_id=dev, device_id_type=MESH
        )

    def arrived(ref, sem):
        remote(ref, ref, sem, sem, ring(vp)).wait_recv()

    def left(ref, sem):
        remote(ref, ref, sem, sem, ring(vp)).wait_send()

    barrier = pltpu.get_barrier_semaphore()

    def greet(dev):
        pl.semaphore_signal(barrier, inc=1, device_id=dev, device_id_type=MESH)

    for d in far_z:
        greet(ring(rem(v + d, 16)))
    for d in far_y:
        greet(at_y(rem(y + d, NY)))
    for d in far_x:
        greet(at_x(rem(x + d, NX)))
    loads = [
        pltpu.make_async_copy(a, b, lsem.at[i])
        for i, (a, b) in enumerate(((qb_h, qb), (qa_h, qa), (cache, cv), (moves_h, moves), (lens_h, lens)))
    ]
    for copy in loads:
        copy.start()
    for copy in loads:
        copy.wait()
    table = read_table(moves)
    out_to = [look(table, lambda m, r=r: (m[0] == g) & (m[1] == r)) for r in range(req)]
    came = [look(table, lambda m, k=k: (m[2] == g) & (m[3] == k)) for k in range(req)]
    length = [lens[g * req + r] for r in range(req)]

    a, _, found = came[1]
    for h in range(NG):
        last = found & (div(a, req) == h)
        qx[h] = jnp.where(last, qa[req + 1].astype(F32), qa[req].astype(F32)).astype(BF16)
    rq[v] = qx[0]
    pl.semaphore_wait(barrier, 15 + NY - 1 + NX - 1)

    def z1(d):
        to = ring(rem(v + d, 16))
        return remote(qx.at[to["group"]], rq.at[v], zs.at[2], zr.at[2], to)

    zq = remote(qb, pb, zs.at[0], zr.at[0], ring(vp))
    zp = remote(qa.at[pl.ds(0, req)], pa, zs.at[1], zr.at[1], ring(vp))
    zq.start()
    for d in far_z:
        z1(d).start()
    zp.start()

    def p1(d, c):
        h = rem(g + d, NG)
        return remote(piece(cv, h, c), st[c].at[g], p1s.at[c], p1r.at[c], at_group(h))

    for c in range(n_cuts):
        loop(0, 7, lambda k: p1((4, 5, 3, 2, 6, 7, 1)[k], c).start())
    keep = [pltpu.make_async_copy(piece(cv, g, c), st[c].at[g], lsem.at[7 + c]) for c in range(n_cuts)]
    for copy in keep:
        copy.start()

    steps = (0, 1, 7, 2, 6, 3, 4, 5)
    bands = (pl.ds(0, 1), pl.ds(1, 2), pl.ds(3, 2), pl.ds(5, 3))

    def slot(d):
        return steps.index(d % NY)

    def ga(u, d):
        band = min(d, NY - d, 3) - 1
        return remote(gq.at[u, x, 0], gq.at[u, x, slot(-d)], as_.at[u], ar.at[u, band], at_y(rem(y + d, NY)))

    def spread(u):
        for d in far_y:
            ga(u, d).start()
        relay(u, 0)

    def relay(u, band):
        part = gq.at[u, x, bands[band]]
        for d in far_x:
            remote(part, part, xs.at[u], xr.at[u, d], at_x(rem(x + d, NX))).start()

    def pass_on(u, band):
        arrived(gq.at[u, x, bands[band + 1]], ar.at[u, band])
        relay(u, band + 1)

    zq.wait()
    for r in range(req):
        for i in range(2):
            mine = zl == i
            bs[0, 4 * i + 2 * r : 4 * i + 2 * r + 2] = jnp.where(mine, qb[r].astype(F32), pb[r].astype(F32))
    gq[0, x, 0] = bs[0].astype(BF16)
    spread(0)
    pass_on(0, 0)
    pass_on(0, 1)

    zp.wait()
    arrived(rq.at[pl.ds(0, 15)], zr.at[2])
    for r in range(req):
        _, target, leaves = out_to[r]
        tg = div(target, req)
        for i in range(2):
            stay = jnp.where(zl == i, qa[r].astype(F32), pa[r].astype(F32))
            away = rq[(div(tg, 2) * 2 + i) * 2 + rem(tg, 2)].astype(F32)
            bs[1, 4 * i + 2 * r : 4 * i + 2 * r + 2] = jnp.where(leaves, away, stay)
    gq[1, x, 0] = bs[1].astype(BF16)
    spread(1)

    n = NY * 8

    def attend(u, sources):
        m = n * len(sources)
        row = lax.broadcasted_iota(jnp.int32, (m, 1), 0)
        second = rem(div(row, 2), 2) == 1
        position = s * shard + lax.broadcasted_iota(jnp.int32, (m, shard), 1)
        blocks = [gq[u, i].astype(F32).reshape(n, width) for i in sources]
        q = (blocks[0] if len(blocks) == 1 else jnp.concatenate(blocks, axis=0)).astype(BF16)
        scores = jnp.where(
            second,
            jnp.dot(q, cv[1], preferred_element_type=F32),
            jnp.dot(q, cv[0], preferred_element_type=F32),
        ) * SCALE
        live = position < jnp.where(second, length[1], length[0])
        masked = jnp.where(live, scores, LOW)
        top = jnp.max(masked, axis=1, keepdims=True)
        weights = jnp.where(live, jnp.exp(masked - top), 0.0)
        total = jnp.sum(weights, axis=1, keepdims=True)
        some = total > 0.0
        safe = jnp.where(some, total, 1.0)
        weights = weights * (1.0 / safe)
        part = None
        for r in range(req):
            mine = jnp.where(second == (r == 1), weights, 0.0).astype(BF16)
            term = lax.dot_general(
                mine, cv[r, :LAT, :], (((1,), (1,)), ((), ())), preferred_element_type=F32
            )
            part = term if part is None else part + term
        part, lse = part.astype(BF16), jnp.where(some, top + jnp.log(safe), LOW)
        return [(part[n * k : n * k + n], to_row(lse[n * k : n * k + n])) for k in range(len(sources))]

    def rc(u, to):
        return (remote(s1.at[u, to], r1.at[u, x], ms.at[u, 0], mr.at[u, 0], at_x(to)),
                remote(t1.at[u, to], u1.at[u, x], ms.at[u, 1], mr.at[u, 1], at_x(to)))

    def each(copies, what):
        for c in copies:
            getattr(c, what)()

    def blocks(u, steps):
        sources = [rem(x + NX - d, NX) for d in steps]
        for d, frm in zip(steps, sources):
            if d:
                arrived(gq.at[u, frm], xr.at[u, d])
        for d, frm, (part, lse) in zip(steps, sources, attend(u, sources)):
            if d:
                s1[u, frm], t1[u, frm] = part, lse
                each(rc(u, frm), "start")
            else:
                r1[u, x], u1[u, x] = part, lse

    def block_from(u, frm):
        arrived(gq.at[u, frm], xr.at[u, rem(x + NX - frm, NX)])
        [(s1[u, frm], t1[u, frm])] = attend(u, [frm])
        each(rc(u, frm), "start")

    def forward(c):
        keep[c].wait()
        arrived(st[c].at[pl.ds(0, NG - 1)], p1r.at[c])

        def pick(i, carry):
            d, k = div(i, req), rem(i, req)
            a, _, found = look(table, lambda m: (m[2] == d) & (m[3] == k))
            value = st[c][div(a, req), rem(a, req)]
            sel[c][d, k] = jnp.where(found, value, jnp.zeros_like(value))
            return carry

        lax.fori_loop(0, NG * req, pick, 0)
        loop(0, 7, lambda k: p2((4, 5, 3, 2, 6, 7, 1)[k], c).start())
        own[c].start()

    def p2(d, c):
        h = rem(g + d, NG)
        return remote(sel[c].at[h], piece(moved, g, c), p2s.at[c], p2r.at[c], at_group(h))

    own = [pltpu.make_async_copy(sel[c].at[g], piece(moved, g, c), lsem.at[7 + n_cuts + c]) for c in range(n_cuts)]

    def re(u, d):
        return remote(s2.at[u, slot(d)], r2.at[u, slot(-d)], ns.at[u], nr.at[u], at_y(rem(y + d, NY)))

    def second_step(u):
        arrived(r1.at[u, pl.ds(0, NX - 1)], mr.at[u, 0])
        arrived(u1.at[u, pl.ds(0, NX - 1)], mr.at[u, 1])
        weights, lse = weigh([u1[u, i] for i in range(NX)])
        part = blend([r1[u, i] for i in range(NX)], [to_column(w, n) for w in weights])
        s2[u, :, :, :LAT] = part.reshape(NY, 8, LAT).astype(BF16)
        s2[u, :, :, LAT:] = tail(to_column(lse, n)).astype(F32).reshape(NY, 8, 128).astype(BF16)
        r2[u, 0] = s2[u, 0]
        for d in far_y:
            re(u, d).start()

    def third_step(u):
        arrived(r2.at[u, pl.ds(0, NY - 1)], nr.at[u])
        part, lse = join([r2[u, i] for i in range(NY)])
        end = tail(lse)
        for i in range(2):
            for r in range(req):
                rows = slice(4 * i + 2 * r, 4 * i + 2 * r + 2)
                s3[u, i, r, :, :LAT] = part[rows].astype(BF16)
                s3[u, i, r, :, LAT:] = end[rows]

    pass_on(0, 2)
    for band in range(3):
        pass_on(1, band)
    blocks(1, (0,))
    forward(0)
    blocks(0, (1, 3, 2, 0))
    forward(1)
    for j in range(NX - 1):
        block_from(1, jnp.where(x <= j, j + 1, j))
    second_step(0)
    forward(2)
    second_step(1)

    def rf(d):
        w = rem(v + d, 16)
        to = ring(w)
        return remote(s4.at[rem(div(w, 2), 2), to["group"]], r3.at[v], os_.at[2], or_.at[2], to)

    fb = remote(s3.at[0, 1 - zl], b3.at[0], os_.at[0], or_.at[0], ring(vp))
    fa = remote(s3.at[1, 1 - zl], b3.at[1], os_.at[1], or_.at[1], ring(vp))
    stays = [pltpu.make_async_copy(s3.at[u, zl], kept.at[u], lsem.at[5]) for u in range(2)]
    fill = pltpu.make_async_copy(s3.at[1, zl, 0], r3.at[v], lsem.at[6])
    third_step(1)
    _, target, leaves = out_to[1]
    for i in range(2):
        for h in range(NG):
            last = leaves & (div(target, req) == h)
            s4[i, h] = jnp.where(last, s3[1, i, 1], s3[1, i, 0])
    for d in far_z:
        rf(d).start()
    fa.start()
    fill.start()
    third_step(0)
    fb.start()
    for copy in stays:
        copy.start()
    fb.wait()
    fa.wait()
    fill.wait()
    pltpu.make_async_copy(kept, kept, lsem.at[5]).wait()
    arrived(r3.at[pl.ds(0, 15)], or_.at[2])
    for c in range(n_cuts):
        own[c].wait()
        arrived(sel[c].at[pl.ds(0, NG - 1)], p2r.at[c])

    left(rq.at[pl.ds(0, 15)], zs.at[2])
    left(r3.at[pl.ds(0, 15)], os_.at[2])
    for u in range(2):
        left(gq.at[u, x, pl.ds(0, NY - 1)], as_.at[u])
        left(gq.at[u, pl.ds(0, NX - 1)], xs.at[u])
        left(s1.at[u, pl.ds(0, NX - 1)], ms.at[u, 0])
        left(t1.at[u, pl.ds(0, NX - 1)], ms.at[u, 1])
        left(s2.at[u, pl.ds(0, NY - 1)], ns.at[u])
    for c in range(n_cuts):
        left(st[c].at[pl.ds(0, NG - 1)], p1s.at[c])
        left(sel[c].at[pl.ds(0, NG - 1)], p2s.at[c])


def finish(lens_h, moves_h, mine_h, b3_h, r3_h, moved, ob_h, lb_h, oa_h, la_h, moved_to,
           lens, moves, mine, b3, r3, ob, lb, oa, la, hold, sems):
    req = ob.shape[0]
    g, zl = lax.axis_index("group"), rem(lax.axis_index("seq"), 2)
    takes = [pltpu.make_async_copy(moved.at[r], hold.at[r], sems.at[0, r]) for r in range(req)]
    puts = [pltpu.make_async_copy(hold.at[r], moved_to.at[r], sems.at[1, r]) for r in range(req)]
    loads = [
        pltpu.make_async_copy(a, b, sems.at[0, req + i])
        for i, (a, b) in enumerate(((lens_h, lens), (moves_h, moves), (mine_h, mine), (b3_h, b3), (r3_h, r3)))
    ]
    stores = [
        pltpu.make_async_copy(a, b, sems.at[1, req + i])
        for i, (a, b) in enumerate(((ob, ob_h), (lb, lb_h), (oa, oa_h), (la, la_h)))
    ]
    for copy in takes + loads:
        copy.start()
    for copy in loads:
        copy.wait()
    table = read_table(moves)
    for r in range(req):
        alive = lens[g * req + r] > 0
        out, lse = join([mine[0, r], b3[0, r]])
        ob[r] = jnp.where(alive, out, 0.0).astype(BF16)
        lb[r : r + 1, :] = to_row(jnp.where(alive, lse, 0.0))[:, 0:2]
        _, _, leaves = look(table, lambda m, r=r: (m[0] == g) & (m[1] == r))
        stays = alive & jnp.logical_not(leaves)
        out, lse = join([mine[1, r], b3[1, r]])
        oa[r] = jnp.where(stays, out, 0.0).astype(BF16)
        la[:, r : r + 1] = jnp.where(stays, lse, 0.0)
    for copy, put in zip(takes, puts):
        copy.wait()
        put.start()
    for k in range(req):
        a, _, found = look(table, lambda m, k=k: (m[2] == g) & (m[3] == k))
        sg = div(a, req)
        out, lse = join([r3[(div(sg, 2) * 2 + i) * 2 + rem(sg, 2)] for i in range(2)])
        alive = found & (lens[a] > 0)
        oa[req + k] = jnp.where(alive, out, 0.0).astype(BF16)
        la[:, req + k : req + k + 1] = jnp.where(alive, lse, 0.0)
    for copy in stores:
        copy.start()
    for copy in stores + puts:
        copy.wait()


def local(cache, lengths, moves, qb, qa):
    req, shard, width = cache.shape
    heads = qb.shape[1]
    n = NY * 8
    wide = LAT + 128
    vm, dma = pltpu.VMEM, pltpu.SemaphoreType.DMA
    hbm = pl.BlockSpec(memory_space=pltpu.HBM)
    shape = jax.ShapeDtypeStruct
    outs = (
        shape((req, heads, LAT), BF16),
        shape((req, heads), F32),
        shape((2 * req, heads, LAT), BF16),
        shape((heads, 2 * req), F32),
        shape((req, width, shard), BF16),
    )
    sent = (
        shape((2, req, heads, wide), BF16),
        shape((2, req, heads, wide), BF16),
        shape((16, heads, wide), BF16),
        outs[4],
    )
    moves = moves.T
    got = pl.pallas_call(
        kernel,
        out_shape=sent,
        in_specs=[hbm] * 5,
        out_specs=(hbm,) * 4,
        scratch_shapes=[
            pltpu.SMEM(lengths.shape, jnp.int32),
            pltpu.SMEM(moves.shape, jnp.int32),
            vm(qb.shape, BF16),
            vm(qa.shape, BF16),
            vm((req, width, shard), BF16),
            *[tuple(vm((NG, req, size, 128), BF16) for size in CUTS)] * 2,
            vm((16, heads, width), BF16),
            vm((NG, heads, width), BF16),
            vm((req, heads, width), BF16),
            vm((req, heads, width), BF16),
            vm((2, 8, width), F32),
            vm((2, NX, NY, 8, width), BF16),
            vm((2, NX, n, LAT), BF16), vm((2, NX, n, LAT), BF16),
            vm((2, NX, 1, 128), F32), vm((2, NX, 1, 128), F32),
            vm((2, NY, 8, wide), BF16), vm((2, NY, 8, wide), BF16),
            vm((2, 2, req, heads, wide), BF16),
            vm((2, NG, heads, wide), BF16),
            dma((7 + 2 * len(CUTS),)),
            *[dma((len(CUTS),))] * 4,
            dma((3,)), dma((3,)),
            dma((2,)), dma((2, 3)),
            dma((2,)), dma((2, NX)),
            dma((2, 2)), dma((2, 2)),
            dma((2,)), dma((2,)),
            dma((3,)), dma((3,)),
        ],
        name="decode_and_move",
        compiler_params=pltpu.CompilerParams(
            collective_id=0, has_side_effects=True, vmem_limit_bytes=63 << 20
        ),
    )(lengths, moves, jnp.transpose(cache, (0, 2, 1)), qb, qa)
    ob, lb, oa, la, moved = pl.pallas_call(
        finish,
        out_shape=outs,
        in_specs=[hbm] * 6,
        out_specs=(hbm,) * 5,
        scratch_shapes=[
            pltpu.SMEM(lengths.shape, jnp.int32),
            pltpu.SMEM(moves.shape, jnp.int32),
            *(vm(o.shape, o.dtype) for o in sent[:3]),
            *(vm(o.shape, o.dtype) for o in outs),
            dma((2, req + 5)),
        ],
        name="finish",
        compiler_params=pltpu.CompilerParams(vmem_limit_bytes=63 << 20),
    )(lengths, moves, *got)
    return ob, lb, oa, la.T, jnp.transpose(moved, (0, 2, 1))


def solution(mesh):
    placed = (P("group", "seq", None), P(), P(), P("group", "seq", None), P("group", "seq", None))
    return jax.shard_map(
        local,
        mesh=mesh,
        in_specs=placed,
        out_specs=(
            P("group", "seq", None),
            P("group", "seq"),
            P("group", "seq", None),
            P("group", "seq"),
            P("group", "seq", None),
        ),
        check_vma=False,
    )
```

```python
import jax
import jax.numpy as jnp
from jax import lax
from jax.experimental import pallas as pl
from jax.experimental.pallas import tpu as pltpu
from jax.sharding import PartitionSpec as P

MESH = pl.DeviceIdType.MESH
LAT = 512
SCALE = 192.0 ** (-0.5)
LOW = -1e30
CUTS = (48, 48, 48)
NX, NY, NZ, NG = 4, 8, 8, 8
F32, BF16 = jnp.float32, jnp.bfloat16


def loop(lo, hi, body):
    for i in range(lo, hi):
        body(i)


def div(a, b):
    return lax.div(a, jnp.int32(b))


def rem(a, b):
    return lax.rem(a, jnp.int32(b))


def to_column(row, n):
    lane = lax.broadcasted_iota(jnp.int32, (n, 128), 1)
    sub = lax.broadcasted_iota(jnp.int32, (n, 128), 0)
    picked = jnp.where(lane == sub, jnp.broadcast_to(row, (n, 128)), 0.0)
    return jnp.sum(picked, axis=1, keepdims=True)


def to_row(column):
    n = column.shape[0]
    lane = lax.broadcasted_iota(jnp.int32, (n, 128), 1)
    sub = lax.broadcasted_iota(jnp.int32, (n, 128), 0)
    spread = jnp.where(lane == sub, jnp.broadcast_to(column, (n, 128)), 0.0)
    return jnp.sum(spread, axis=0, keepdims=True)


def weigh(stats):
    top = stats[0]
    for s in stats[1:]:
        top = jnp.maximum(top, s)
    weights = [jnp.exp(s - top) for s in stats]
    total = weights[0]
    for w in weights[1:]:
        total = total + w
    scale = 1.0 / total
    return [w * scale for w in weights], top + jnp.log(total)


def blend(parts, columns):
    out = None
    for part, w in zip(parts, columns):
        term = w * part.astype(F32)
        out = term if out is None else out + term
    return out


def tail(column):
    n = column.shape[0]
    high = column.astype(BF16).astype(F32)
    rest = column - high
    mid = rest.astype(BF16).astype(F32)
    lane = lax.broadcasted_iota(jnp.int32, (n, 128), 1)
    terms = jnp.where(lane == 0, high, jnp.where(lane == 1, mid, jnp.where(lane == 2, rest - mid, 0.0)))
    return terms.astype(BF16)


def untail(block):
    return jnp.sum(block.astype(F32), axis=1, keepdims=True)


def join(blocks):
    weights, lse = weigh([untail(b[:, LAT:]) for b in blocks])
    return blend([b[:, :LAT] for b in blocks], weights), lse


def look(table, match):
    a = b = c = jnp.int32(0)
    for m in table:
        hit = match(m)
        a = a + jnp.where(hit, m[0] * 2 + m[1], 0)
        b = b + jnp.where(hit, m[2] * 2 + m[3], 0)
        c = c + jnp.where(hit, 1, 0)
    return a, b, c > 0


def read_table(moves):
    return [[moves[c, i] for c in range(4)] for i in range(moves.shape[1])]


def kernel(lens_h, moves_h, cache, qb_h, qa_h, kept, b3, r3, moved,
           lens, moves, plan, qb, qa, cv, st, sel, rq, qx, pb, pa, bs, gq,
           s1, r1, t1, u1, s2, r2, s3, s4,
           lsem, p1s, p1r, p2s, p2r, zs, zr, as_, ar, xs, xr, ms, mr, ns, nr, os_, or_):
    req, width, shard = cv.shape
    high = width // (NG // 2)
    cuts, low = [], 0
    for ref in st:
        cuts.append((low, ref.shape[2]))
        low += ref.shape[2]
    n_cuts = len(cuts)
    g, s = lax.axis_index("group"), lax.axis_index("seq")
    zh, core = div(g, 2), rem(g, 2)
    x, y, zl = div(s, 2 * NY), rem(div(s, 2), NY), rem(s, 2)
    v = (zh * 2 + zl) * 2 + core

    def ring(w):
        z, c = div(w, 2), rem(w, 2)
        return {"group": div(z, 2) * 2 + c, "seq": (x * NY + y) * 2 + rem(z, 2)}

    def at_group(h):
        return {"group": h, "seq": s}

    def at_x(i):
        return {"group": g, "seq": (i * NY + y) * 2 + zl}

    def at_y(i):
        return {"group": g, "seq": (x * NY + i) * 2 + zl}

    vp = ((zh * 2 + (1 - zl)) * 2) + core
    far_x, far_y, far_z = (2, 1, 3), (4, 3, 5, 2, 6, 1, 7), (8, 9, 7, 6, 10, 5, 11, 4, 12, 3, 13, 2, 14, 1, 15)
    near_x = (1, 3, 2)

    def piece(ref, h, c):
        low, size = cuts[c]
        at = pl.multiple_of(div(h, 2) * high + low, 16)
        return ref.at[:, pl.ds(at, size), pl.ds(pl.multiple_of(rem(h, 2) * 128, 128), 128)]

    def remote(src, dst, ss, rs, dev):
        return pltpu.make_async_remote_copy(
            src_ref=src, dst_ref=dst, send_sem=ss, recv_sem=rs, device_id=dev, device_id_type=MESH
        )

    def arrived(ref, sem):
        remote(ref, ref, sem, sem, ring(vp)).wait_recv()

    def left(ref, sem):
        remote(ref, ref, sem, sem, ring(vp)).wait_send()

    barrier = pltpu.get_barrier_semaphore()

    def greet(dev):
        pl.semaphore_signal(barrier, inc=1, device_id=dev, device_id_type=MESH)

    for d in far_z:
        greet(ring(rem(v + d, 16)))
    for d in far_y:
        greet(at_y(rem(y + d, NY)))
    for d in far_x:
        greet(at_x(rem(x + d, NX)))
    loads = [
        pltpu.make_async_copy(a, b, lsem.at[i])
        for i, (a, b) in enumerate(((qb_h, qb), (qa_h, qa), (cache, cv), (moves_h, moves), (lens_h, lens)))
    ]
    for copy in loads:
        copy.start()
    for copy in loads:
        copy.wait()
    table = read_table(moves)
    out_to = [look(table, lambda m, r=r: (m[0] == g) & (m[1] == r)) for r in range(req)]
    came = [look(table, lambda m, k=k: (m[2] == g) & (m[3] == k)) for k in range(req)]
    length = [lens[g * req + r] for r in range(req)]

    def note(i, carry):
        a, _, found = look(table, lambda m: m[2] * req + m[3] == i)
        plan[0, i], plan[1, i], plan[2, i] = div(a, req), rem(a, req), found.astype(jnp.int32)
        return carry

    lax.fori_loop(0, NG * req, note, 0)

    a, _, found = came[1]
    for h in range(NG):
        last = found & (div(a, req) == h)
        qx[h] = jnp.where(last, qa[req + 1].astype(F32), qa[req].astype(F32)).astype(BF16)
    rq[v] = qx[0]
    pl.semaphore_wait(barrier, 15 + NY - 1 + NX - 1)

    def z1(d):
        to = ring(rem(v + d, 16))
        return remote(qx.at[to["group"]], rq.at[v], zs.at[2], zr.at[2], to)

    zq = remote(qb, pb, zs.at[0], zr.at[0], ring(vp))
    zp = remote(qa.at[pl.ds(0, req)], pa, zs.at[1], zr.at[1], ring(vp))
    zq.start()
    for d in far_z:
        z1(d).start()
    zp.start()

    def p1(d, c):
        h = rem(g + d, NG)
        return remote(piece(cv, h, c), st[c].at[g], p1s.at[c], p1r.at[c], at_group(h))

    for c in range(n_cuts):
        loop(0, 7, lambda k: p1((4, 5, 3, 2, 6, 7, 1)[k], c).start())
    keep = [pltpu.make_async_copy(piece(cv, g, c), st[c].at[g], lsem.at[7 + c]) for c in range(n_cuts)]
    for copy in keep:
        copy.start()

    steps = (0, 1, 7, 2, 6, 3, 4, 5)
    bands = (pl.ds(0, 1), pl.ds(1, 2), pl.ds(3, 2), pl.ds(5, 3))

    def slot(d):
        return steps.index(d % NY)

    def ga(u, d):
        band = min(d, NY - d, 3) - 1
        return remote(gq.at[u, x, 0], gq.at[u, x, slot(-d)], as_.at[u], ar.at[u, band], at_y(rem(y + d, NY)))

    def spread(u):
        for d in far_y:
            ga(u, d).start()
        relay(u, 0)

    def relay(u, band):
        part = gq.at[u, x, bands[band]]
        for d in far_x:
            remote(part, part, xs.at[u], xr.at[u, d], at_x(rem(x + d, NX))).start()

    def pass_on(u, band):
        arrived(gq.at[u, x, bands[band + 1]], ar.at[u, band])
        relay(u, band + 1)

    zq.wait()
    for r in range(req):
        for i in range(2):
            mine = zl == i
            bs[0, 4 * i + 2 * r : 4 * i + 2 * r + 2] = jnp.where(mine, qb[r].astype(F32), pb[r].astype(F32))
    gq[0, x, 0] = bs[0].astype(BF16)
    spread(0)
    pass_on(0, 0)
    pass_on(0, 1)

    zp.wait()
    arrived(rq.at[pl.ds(0, 15)], zr.at[2])
    for r in range(req):
        _, target, leaves = out_to[r]
        tg = div(target, req)
        for i in range(2):
            stay = jnp.where(zl == i, qa[r].astype(F32), pa[r].astype(F32))
            away = rq[(div(tg, 2) * 2 + i) * 2 + rem(tg, 2)].astype(F32)
            bs[1, 4 * i + 2 * r : 4 * i + 2 * r + 2] = jnp.where(leaves, away, stay)
    gq[1, x, 0] = bs[1].astype(BF16)
    spread(1)

    n = NY * 8

    def attend(u, sources):
        m = n * len(sources)
        row = lax.broadcasted_iota(jnp.int32, (m, 1), 0)
        second = rem(div(row, 2), 2) == 1
        position = s * shard + lax.broadcasted_iota(jnp.int32, (m, shard), 1)
        blocks = [gq[u, i].astype(F32).reshape(n, width) for i in sources]
        q = (blocks[0] if len(blocks) == 1 else jnp.concatenate(blocks, axis=0)).astype(BF16)
        scores = jnp.where(
            second,
            jnp.dot(q, cv[1], preferred_element_type=F32),
            jnp.dot(q, cv[0], preferred_element_type=F32),
        ) * SCALE
        live = position < jnp.where(second, length[1], length[0])
        masked = jnp.where(live, scores, LOW)
        top = jnp.max(masked, axis=1, keepdims=True)
        weights = jnp.where(live, jnp.exp(masked - top), 0.0)
        total = jnp.sum(weights, axis=1, keepdims=True)
        some = total > 0.0
        safe = jnp.where(some, total, 1.0)
        weights = weights * (1.0 / safe)
        part = None
        for r in range(req):
            mine = jnp.where(second == (r == 1), weights, 0.0).astype(BF16)
            term = lax.dot_general(
                mine, cv[r, :LAT, :], (((1,), (1,)), ((), ())), preferred_element_type=F32
            )
            part = term if part is None else part + term
        part, lse = part.astype(BF16), jnp.where(some, top + jnp.log(safe), LOW)
        return [(part[n * k : n * k + n], to_row(lse[n * k : n * k + n])) for k in range(len(sources))]

    def rc(u, to):
        return (remote(s1.at[u, to], r1.at[u, x], ms.at[u, 0], mr.at[u, 0], at_x(to)),
                remote(t1.at[u, to], u1.at[u, x], ms.at[u, 1], mr.at[u, 1], at_x(to)))

    def each(copies, what):
        for c in copies:
            getattr(c, what)()

    def blocks(u, steps):
        sources = [rem(x + NX - d, NX) for d in steps]
        for d, frm in zip(steps, sources):
            if d:
                arrived(gq.at[u, frm], xr.at[u, d])
        for d, frm, (part, lse) in zip(steps, sources, attend(u, sources)):
            if d:
                s1[u, frm], t1[u, frm] = part, lse
                each(rc(u, frm), "start")
            else:
                r1[u, x], u1[u, x] = part, lse

    def block_from(u, frm):
        arrived(gq.at[u, frm], xr.at[u, rem(x + NX - frm, NX)])
        [(s1[u, frm], t1[u, frm])] = attend(u, [frm])
        each(rc(u, frm), "start")

    def forward(c):
        keep[c].wait()
        arrived(st[c].at[pl.ds(0, NG - 1)], p1r.at[c])

        def pick(i, carry):
            value = st[c][plan[0, i], plan[1, i]]
            sel[c][div(i, req), rem(i, req)] = jnp.where(plan[2, i] > 0, value, jnp.zeros_like(value))
            return carry

        lax.fori_loop(0, NG * req, pick, 0)
        loop(0, 7, lambda k: p2((4, 5, 3, 2, 6, 7, 1)[k], c).start())
        own[c].start()

    def p2(d, c):
        h = rem(g + d, NG)
        return remote(sel[c].at[h], piece(moved, g, c), p2s.at[c], p2r.at[c], at_group(h))

    own = [pltpu.make_async_copy(sel[c].at[g], piece(moved, g, c), lsem.at[7 + n_cuts + c]) for c in range(n_cuts)]

    def re(u, d):
        return remote(s2.at[u, slot(d)], r2.at[u, slot(-d)], ns.at[u], nr.at[u], at_y(rem(y + d, NY)))

    def second_step(u):
        arrived(r1.at[u, pl.ds(0, NX - 1)], mr.at[u, 0])
        arrived(u1.at[u, pl.ds(0, NX - 1)], mr.at[u, 1])
        weights, lse = weigh([u1[u, i] for i in range(NX)])
        part = blend([r1[u, i] for i in range(NX)], [to_column(w, n) for w in weights])
        s2[u, :, :, :LAT] = part.reshape(NY, 8, LAT).astype(BF16)
        s2[u, :, :, LAT:] = tail(to_column(lse, n)).astype(F32).reshape(NY, 8, 128).astype(BF16)
        r2[u, 0] = s2[u, 0]
        for d in far_y:
            re(u, d).start()

    def third_step(u):
        arrived(r2.at[u, pl.ds(0, NY - 1)], nr.at[u])
        part, lse = join([r2[u, i] for i in range(NY)])
        end = tail(lse)
        for i in range(2):
            for r in range(req):
                rows = slice(4 * i + 2 * r, 4 * i + 2 * r + 2)
                s3[u, i, r, :, :LAT] = part[rows].astype(BF16)
                s3[u, i, r, :, LAT:] = end[rows]

    pass_on(0, 2)
    for band in range(3):
        pass_on(1, band)
    blocks(1, (0,))
    forward(0)
    blocks(0, (1, 3, 2, 0))
    for j in range(NX - 1):
        block_from(1, jnp.where(x <= j, j + 1, j))
    forward(1)
    second_step(0)
    forward(2)
    second_step(1)

    def rf(d):
        w = rem(v + d, 16)
        to = ring(w)
        return remote(s4.at[rem(div(w, 2), 2), to["group"]], r3.at[v], os_.at[2], or_.at[2], to)

    fb = remote(s3.at[0, 1 - zl], b3.at[0], os_.at[0], or_.at[0], ring(vp))
    fa = remote(s3.at[1, 1 - zl], b3.at[1], os_.at[1], or_.at[1], ring(vp))
    stays = [pltpu.make_async_copy(s3.at[u, zl], kept.at[u], lsem.at[5]) for u in range(2)]
    fill = pltpu.make_async_copy(s3.at[1, zl, 0], r3.at[v], lsem.at[6])
    third_step(1)
    _, target, leaves = out_to[1]
    for i in range(2):
        for h in range(NG):
            last = leaves & (div(target, req) == h)
            s4[i, h] = jnp.where(last, s3[1, i, 1], s3[1, i, 0])
    for d in far_z:
        rf(d).start()
    fa.start()
    fill.start()
    third_step(0)
    fb.start()
    for copy in stays:
        copy.start()
    fb.wait()
    fa.wait()
    fill.wait()
    pltpu.make_async_copy(kept, kept, lsem.at[5]).wait()
    arrived(r3.at[pl.ds(0, 15)], or_.at[2])
    for c in range(n_cuts):
        own[c].wait()
        arrived(sel[c].at[pl.ds(0, NG - 1)], p2r.at[c])

    left(rq.at[pl.ds(0, 15)], zs.at[2])
    left(r3.at[pl.ds(0, 15)], os_.at[2])
    for u in range(2):
        left(gq.at[u, x, pl.ds(0, NY - 1)], as_.at[u])
        left(gq.at[u, pl.ds(0, NX - 1)], xs.at[u])
        left(s1.at[u, pl.ds(0, NX - 1)], ms.at[u, 0])
        left(t1.at[u, pl.ds(0, NX - 1)], ms.at[u, 1])
        left(s2.at[u, pl.ds(0, NY - 1)], ns.at[u])
    for c in range(n_cuts):
        left(st[c].at[pl.ds(0, NG - 1)], p1s.at[c])
        left(sel[c].at[pl.ds(0, NG - 1)], p2s.at[c])


def finish(lens_h, moves_h, mine_h, b3_h, r3_h, moved, ob_h, lb_h, oa_h, la_h, moved_to,
           lens, moves, mine, b3, r3, ob, lb, oa, la, hold, sems):
    req = ob.shape[0]
    g, zl = lax.axis_index("group"), rem(lax.axis_index("seq"), 2)
    takes = [pltpu.make_async_copy(moved.at[r], hold.at[r], sems.at[0, r]) for r in range(req)]
    puts = [pltpu.make_async_copy(hold.at[r], moved_to.at[r], sems.at[1, r]) for r in range(req)]
    loads = [
        pltpu.make_async_copy(a, b, sems.at[0, req + i])
        for i, (a, b) in enumerate(((lens_h, lens), (moves_h, moves), (mine_h, mine), (b3_h, b3), (r3_h, r3)))
    ]
    stores = [
        pltpu.make_async_copy(a, b, sems.at[1, req + i])
        for i, (a, b) in enumerate(((ob, ob_h), (lb, lb_h), (oa, oa_h), (la, la_h)))
    ]
    for copy in takes + loads:
        copy.start()
    for copy in loads:
        copy.wait()
    table = read_table(moves)
    for r in range(req):
        alive = lens[g * req + r] > 0
        out, lse = join([mine[0, r], b3[0, r]])
        ob[r] = jnp.where(alive, out, 0.0).astype(BF16)
        lb[r : r + 1, :] = to_row(jnp.where(alive, lse, 0.0))[:, 0:2]
        _, _, leaves = look(table, lambda m, r=r: (m[0] == g) & (m[1] == r))
        stays = alive & jnp.logical_not(leaves)
        out, lse = join([mine[1, r], b3[1, r]])
        oa[r] = jnp.where(stays, out, 0.0).astype(BF16)
        la[:, r : r + 1] = jnp.where(stays, lse, 0.0)
    for copy, put in zip(takes, puts):
        copy.wait()
        put.start()
    for k in range(req):
        a, _, found = look(table, lambda m, k=k: (m[2] == g) & (m[3] == k))
        sg = div(a, req)
        out, lse = join([r3[(div(sg, 2) * 2 + i) * 2 + rem(sg, 2)] for i in range(2)])
        alive = found & (lens[a] > 0)
        oa[req + k] = jnp.where(alive, out, 0.0).astype(BF16)
        la[:, req + k : req + k + 1] = jnp.where(alive, lse, 0.0)
    for copy in stores:
        copy.start()
    for copy in stores + puts:
        copy.wait()


def local(cache, lengths, moves, qb, qa):
    req, shard, width = cache.shape
    heads = qb.shape[1]
    n = NY * 8
    wide = LAT + 128
    vm, dma = pltpu.VMEM, pltpu.SemaphoreType.DMA
    hbm = pl.BlockSpec(memory_space=pltpu.HBM)
    shape = jax.ShapeDtypeStruct
    outs = (
        shape((req, heads, LAT), BF16),
        shape((req, heads), F32),
        shape((2 * req, heads, LAT), BF16),
        shape((heads, 2 * req), F32),
        shape((req, width, shard), BF16),
    )
    sent = (
        shape((2, req, heads, wide), BF16),
        shape((2, req, heads, wide), BF16),
        shape((16, heads, wide), BF16),
        outs[4],
    )
    moves = moves.T
    got = pl.pallas_call(
        kernel,
        out_shape=sent,
        in_specs=[hbm] * 5,
        out_specs=(hbm,) * 4,
        scratch_shapes=[
            pltpu.SMEM(lengths.shape, jnp.int32),
            pltpu.SMEM(moves.shape, jnp.int32),
            pltpu.SMEM((3, NG * req), jnp.int32),
            vm(qb.shape, BF16),
            vm(qa.shape, BF16),
            vm((req, width, shard), BF16),
            *[tuple(vm((NG, req, size, 128), BF16) for size in CUTS)] * 2,
            vm((16, heads, width), BF16),
            vm((NG, heads, width), BF16),
            vm((req, heads, width), BF16),
            vm((req, heads, width), BF16),
            vm((2, 8, width), F32),
            vm((2, NX, NY, 8, width), BF16),
            vm((2, NX, n, LAT), BF16), vm((2, NX, n, LAT), BF16),
            vm((2, NX, 1, 128), F32), vm((2, NX, 1, 128), F32),
            vm((2, NY, 8, wide), BF16), vm((2, NY, 8, wide), BF16),
            vm((2, 2, req, heads, wide), BF16),
            vm((2, NG, heads, wide), BF16),
            dma((7 + 2 * len(CUTS),)),
            *[dma((len(CUTS),))] * 4,
            dma((3,)), dma((3,)),
            dma((2,)), dma((2, 3)),
            dma((2,)), dma((2, NX)),
            dma((2, 2)), dma((2, 2)),
            dma((2,)), dma((2,)),
            dma((3,)), dma((3,)),
        ],
        name="decode_and_move",
        compiler_params=pltpu.CompilerParams(
            collective_id=0, has_side_effects=True, vmem_limit_bytes=63 << 20
        ),
    )(lengths, moves, jnp.transpose(cache, (0, 2, 1)), qb, qa)
    ob, lb, oa, la, moved = pl.pallas_call(
        finish,
        out_shape=outs,
        in_specs=[hbm] * 6,
        out_specs=(hbm,) * 5,
        scratch_shapes=[
            pltpu.SMEM(lengths.shape, jnp.int32),
            pltpu.SMEM(moves.shape, jnp.int32),
            *(vm(o.shape, o.dtype) for o in sent[:3]),
            *(vm(o.shape, o.dtype) for o in outs),
            dma((2, req + 5)),
        ],
        name="finish",
        compiler_params=pltpu.CompilerParams(vmem_limit_bytes=63 << 20),
    )(lengths, moves, *got)
    return ob, lb, oa, la.T, jnp.transpose(moved, (0, 2, 1))


def solution(mesh):
    placed = (P("group", "seq", None), P(), P(), P("group", "seq", None), P("group", "seq", None))
    return jax.shard_map(
        local,
        mesh=mesh,
        in_specs=placed,
        out_specs=(
            P("group", "seq", None),
            P("group", "seq"),
            P("group", "seq", None),
            P("group", "seq"),
            P("group", "seq", None),
        ),
        check_vma=False,
    )
```

```python
import jax
import jax.numpy as jnp
from jax import lax
from jax.experimental import pallas as pl
from jax.experimental.pallas import tpu as pltpu
from jax.sharding import PartitionSpec as P

MESH = pl.DeviceIdType.MESH
LAT = 512
SCALE = 192.0 ** (-0.5)
LOW = -1e30
CUTS = (48, 48, 48)
NX, NY, NZ, NG = 4, 8, 8, 8
F32, BF16 = jnp.float32, jnp.bfloat16


def loop(lo, hi, body):
    for i in range(lo, hi):
        body(i)


def div(a, b):
    return lax.div(a, jnp.int32(b))


def rem(a, b):
    return lax.rem(a, jnp.int32(b))


def to_column(row, n):
    lane = lax.broadcasted_iota(jnp.int32, (n, 128), 1)
    sub = lax.broadcasted_iota(jnp.int32, (n, 128), 0)
    picked = jnp.where(lane == sub, jnp.broadcast_to(row, (n, 128)), 0.0)
    return jnp.sum(picked, axis=1, keepdims=True)


def to_row(column):
    n = column.shape[0]
    lane = lax.broadcasted_iota(jnp.int32, (n, 128), 1)
    sub = lax.broadcasted_iota(jnp.int32, (n, 128), 0)
    spread = jnp.where(lane == sub, jnp.broadcast_to(column, (n, 128)), 0.0)
    return jnp.sum(spread, axis=0, keepdims=True)


def weigh(stats):
    top = stats[0]
    for s in stats[1:]:
        top = jnp.maximum(top, s)
    weights = [jnp.exp(s - top) for s in stats]
    total = weights[0]
    for w in weights[1:]:
        total = total + w
    scale = 1.0 / total
    return [w * scale for w in weights], top + jnp.log(total)


def blend(parts, columns):
    out = None
    for part, w in zip(parts, columns):
        term = w * part.astype(F32)
        out = term if out is None else out + term
    return out


def tail(column):
    n = column.shape[0]
    high = column.astype(BF16).astype(F32)
    rest = column - high
    mid = rest.astype(BF16).astype(F32)
    lane = lax.broadcasted_iota(jnp.int32, (n, 128), 1)
    terms = jnp.where(lane == 0, high, jnp.where(lane == 1, mid, jnp.where(lane == 2, rest - mid, 0.0)))
    return terms.astype(BF16)


def untail(block):
    return jnp.sum(block.astype(F32), axis=1, keepdims=True)


def join(blocks):
    weights, lse = weigh([untail(b[:, LAT:]) for b in blocks])
    return blend([b[:, :LAT] for b in blocks], weights), lse


def look(table, match):
    a = b = c = jnp.int32(0)
    for m in table:
        hit = match(m)
        a = a + jnp.where(hit, m[0] * 2 + m[1], 0)
        b = b + jnp.where(hit, m[2] * 2 + m[3], 0)
        c = c + jnp.where(hit, 1, 0)
    return a, b, c > 0


def read_table(moves):
    return [[moves[c, i] for c in range(4)] for i in range(moves.shape[1])]


def kernel(lens_h, moves_h, cache, qb_h, qa_h, kept, b3, r3, moved,
           lens, moves, plan, qb, qa, cv, st, sel, rq, qx, pb, pa, bs, gq,
           s1, r1, t1, u1, s2, r2, s3, s4,
           lsem, p1s, p1r, p2s, p2r, zs, zr, as_, ar, xs, xr, ms, mr, ns, nr, os_, or_):
    req, width, shard = cv.shape
    high = width // (NG // 2)
    cuts, low = [], 0
    for ref in st:
        cuts.append((low, ref.shape[2]))
        low += ref.shape[2]
    n_cuts = len(cuts)
    g, s = lax.axis_index("group"), lax.axis_index("seq")
    zh, core = div(g, 2), rem(g, 2)
    x, y, zl = div(s, 2 * NY), rem(div(s, 2), NY), rem(s, 2)
    v = (zh * 2 + zl) * 2 + core

    def ring(w):
        z, c = div(w, 2), rem(w, 2)
        return {"group": div(z, 2) * 2 + c, "seq": (x * NY + y) * 2 + rem(z, 2)}

    def at_group(h):
        return {"group": h, "seq": s}

    def at_x(i):
        return {"group": g, "seq": (i * NY + y) * 2 + zl}

    def at_y(i):
        return {"group": g, "seq": (x * NY + i) * 2 + zl}

    vp = ((zh * 2 + (1 - zl)) * 2) + core
    far_x, far_y, far_z = (2, 1, 3), (4, 3, 5, 2, 6, 1, 7), (8, 9, 7, 6, 10, 5, 11, 4, 12, 3, 13, 2, 14, 1, 15)
    near_x = (1, 3, 2)

    def piece(ref, h, c):
        low, size = cuts[c]
        at = pl.multiple_of(div(h, 2) * high + low, 16)
        return ref.at[:, pl.ds(at, size), pl.ds(pl.multiple_of(rem(h, 2) * 128, 128), 128)]

    def remote(src, dst, ss, rs, dev):
        return pltpu.make_async_remote_copy(
            src_ref=src, dst_ref=dst, send_sem=ss, recv_sem=rs, device_id=dev, device_id_type=MESH
        )

    def arrived(ref, sem):
        remote(ref, ref, sem, sem, ring(vp)).wait_recv()

    def left(ref, sem):
        remote(ref, ref, sem, sem, ring(vp)).wait_send()

    barrier = pltpu.get_barrier_semaphore()

    def greet(dev):
        pl.semaphore_signal(barrier, inc=1, device_id=dev, device_id_type=MESH)

    for d in far_z[:6]:
        greet(ring(rem(v + d, 16)))
    for d in far_y:
        greet(at_y(rem(y + d, NY)))
    for d in far_z[6:]:
        greet(ring(rem(v + d, 16)))
    for d in far_x:
        greet(at_x(rem(x + d, NX)))
    loads = [
        pltpu.make_async_copy(a, b, lsem.at[i])
        for i, (a, b) in enumerate(((qb_h, qb), (qa_h, qa), (cache, cv), (moves_h, moves), (lens_h, lens)))
    ]
    for copy in loads:
        copy.start()
    for copy in loads:
        copy.wait()
    table = read_table(moves)
    out_to = [look(table, lambda m, r=r: (m[0] == g) & (m[1] == r)) for r in range(req)]
    came = [look(table, lambda m, k=k: (m[2] == g) & (m[3] == k)) for k in range(req)]
    length = [lens[g * req + r] for r in range(req)]

    def note(i, carry):
        a, _, found = look(table, lambda m: m[2] * req + m[3] == i)
        plan[0, i], plan[1, i], plan[2, i] = div(a, req), rem(a, req), found.astype(jnp.int32)
        return carry

    lax.fori_loop(0, NG * req, note, 0)

    a, _, found = came[1]
    for h in range(NG):
        last = found & (div(a, req) == h)
        qx[h] = jnp.where(last, qa[req + 1].astype(F32), qa[req].astype(F32)).astype(BF16)
    rq[v] = qx[0]
    pl.semaphore_wait(barrier, 15 + NY - 1 + NX - 1)

    def z1(d):
        to = ring(rem(v + d, 16))
        return remote(qx.at[to["group"]], rq.at[v], zs.at[2], zr.at[2], to)

    zq = remote(qb, pb, zs.at[0], zr.at[0], ring(vp))
    zp = remote(qa.at[pl.ds(0, req)], pa, zs.at[1], zr.at[1], ring(vp))
    zq.start()
    for d in far_z:
        z1(d).start()
    zp.start()

    def p1(d, c):
        h = rem(g + d, NG)
        return remote(piece(cv, h, c), st[c].at[g], p1s.at[c], p1r.at[c], at_group(h))

    for c in range(n_cuts):
        loop(0, 7, lambda k: p1((4, 5, 3, 2, 6, 7, 1)[k], c).start())
    keep = [pltpu.make_async_copy(piece(cv, g, c), st[c].at[g], lsem.at[7 + c]) for c in range(n_cuts)]
    for copy in keep:
        copy.start()

    steps = (0, 1, 7, 2, 6, 3, 4, 5)
    bands = (pl.ds(0, 1), pl.ds(1, 2), pl.ds(3, 2), pl.ds(5, 3))

    def slot(d):
        return steps.index(d % NY)

    def ga(u, d):
        band = min(d, NY - d, 3) - 1
        return remote(gq.at[u, x, 0], gq.at[u, x, slot(-d)], as_.at[u], ar.at[u, band], at_y(rem(y + d, NY)))

    def spread(u):
        for d in far_y:
            ga(u, d).start()
        relay(u, 0)

    def relay(u, band):
        part = gq.at[u, x, bands[band]]
        for d in far_x:
            remote(part, part, xs.at[u], xr.at[u, d], at_x(rem(x + d, NX))).start()

    def pass_on(u, band):
        arrived(gq.at[u, x, bands[band + 1]], ar.at[u, band])
        relay(u, band + 1)

    zq.wait()
    for r in range(req):
        for i in range(2):
            mine = zl == i
            bs[0, 4 * i + 2 * r : 4 * i + 2 * r + 2] = jnp.where(mine, qb[r].astype(F32), pb[r].astype(F32))
    gq[0, x, 0] = bs[0].astype(BF16)
    spread(0)
    pass_on(0, 0)
    pass_on(0, 1)

    zp.wait()
    arrived(rq.at[pl.ds(0, 15)], zr.at[2])
    for r in range(req):
        _, target, leaves = out_to[r]
        tg = div(target, req)
        for i in range(2):
            stay = jnp.where(zl == i, qa[r].astype(F32), pa[r].astype(F32))
            away = rq[(div(tg, 2) * 2 + i) * 2 + rem(tg, 2)].astype(F32)
            bs[1, 4 * i + 2 * r : 4 * i + 2 * r + 2] = jnp.where(leaves, away, stay)
    gq[1, x, 0] = bs[1].astype(BF16)
    spread(1)

    n = NY * 8

    def attend(u, sources):
        m = n * len(sources)
        row = lax.broadcasted_iota(jnp.int32, (m, 1), 0)
        second = rem(div(row, 2), 2) == 1
        position = s * shard + lax.broadcasted_iota(jnp.int32, (m, shard), 1)
        blocks = [gq[u, i].astype(F32).reshape(n, width) for i in sources]
        q = (blocks[0] if len(blocks) == 1 else jnp.concatenate(blocks, axis=0)).astype(BF16)
        scores = jnp.where(
            second,
            jnp.dot(q, cv[1], preferred_element_type=F32),
            jnp.dot(q, cv[0], preferred_element_type=F32),
        ) * SCALE
        live = position < jnp.where(second, length[1], length[0])
        masked = jnp.where(live, scores, LOW)
        top = jnp.max(masked, axis=1, keepdims=True)
        weights = jnp.where(live, jnp.exp(masked - top), 0.0)
        total = jnp.sum(weights, axis=1, keepdims=True)
        some = total > 0.0
        safe = jnp.where(some, total, 1.0)
        weights = weights * (1.0 / safe)
        part = None
        for r in range(req):
            mine = jnp.where(second == (r == 1), weights, 0.0).astype(BF16)
            term = lax.dot_general(
                mine, cv[r, :LAT, :], (((1,), (1,)), ((), ())), preferred_element_type=F32
            )
            part = term if part is None else part + term
        part, lse = part.astype(BF16), jnp.where(some, top + jnp.log(safe), LOW)
        return [(part[n * k : n * k + n], to_row(lse[n * k : n * k + n])) for k in range(len(sources))]

    def rc(u, to):
        return (remote(s1.at[u, to], r1.at[u, x], ms.at[u, 0], mr.at[u, 0], at_x(to)),
                remote(t1.at[u, to], u1.at[u, x], ms.at[u, 1], mr.at[u, 1], at_x(to)))

    def each(copies, what):
        for c in copies:
            getattr(c, what)()

    def blocks(u, steps):
        sources = [rem(x + NX - d, NX) for d in steps]
        for d, frm in zip(steps, sources):
            if d:
                arrived(gq.at[u, frm], xr.at[u, d])
        for d, frm, (part, lse) in zip(steps, sources, attend(u, sources)):
            if d:
                s1[u, frm], t1[u, frm] = part, lse
                each(rc(u, frm), "start")
            else:
                r1[u, x], u1[u, x] = part, lse

    def block_from(u, frm):
        arrived(gq.at[u, frm], xr.at[u, rem(x + NX - frm, NX)])
        [(s1[u, frm], t1[u, frm])] = attend(u, [frm])
        each(rc(u, frm), "start")

    def forward(c):
        keep[c].wait()
        arrived(st[c].at[pl.ds(0, NG - 1)], p1r.at[c])

        def pick(i, carry):
            value = st[c][plan[0, i], plan[1, i]]
            sel[c][div(i, req), rem(i, req)] = jnp.where(plan[2, i] > 0, value, jnp.zeros_like(value))
            return carry

        lax.fori_loop(0, NG * req, pick, 0)
        loop(0, 7, lambda k: p2((4, 5, 3, 2, 6, 7, 1)[k], c).start())
        own[c].start()

    def p2(d, c):
        h = rem(g + d, NG)
        return remote(sel[c].at[h], piece(moved, g, c), p2s.at[c], p2r.at[c], at_group(h))

    own = [pltpu.make_async_copy(sel[c].at[g], piece(moved, g, c), lsem.at[7 + n_cuts + c]) for c in range(n_cuts)]

    def re(u, d):
        return remote(s2.at[u, slot(d)], r2.at[u, slot(-d)], ns.at[u], nr.at[u], at_y(rem(y + d, NY)))

    def second_step(u):
        arrived(r1.at[u, pl.ds(0, NX - 1)], mr.at[u, 0])
        arrived(u1.at[u, pl.ds(0, NX - 1)], mr.at[u, 1])
        weights, lse = weigh([u1[u, i] for i in range(NX)])
        part = blend([r1[u, i] for i in range(NX)], [to_column(w, n) for w in weights])
        s2[u, :, :, :LAT] = part.reshape(NY, 8, LAT).astype(BF16)
        s2[u, :, :, LAT:] = tail(to_column(lse, n)).astype(F32).reshape(NY, 8, 128).astype(BF16)
        r2[u, 0] = s2[u, 0]
        for d in far_y:
            re(u, d).start()

    def third_step(u):
        arrived(r2.at[u, pl.ds(0, NY - 1)], nr.at[u])
        part, lse = join([r2[u, i] for i in range(NY)])
        end = tail(lse)
        for i in range(2):
            for r in range(req):
                rows = slice(4 * i + 2 * r, 4 * i + 2 * r + 2)
                s3[u, i, r, :, :LAT] = part[rows].astype(BF16)
                s3[u, i, r, :, LAT:] = end[rows]

    pass_on(0, 2)
    for band in range(3):
        pass_on(1, band)
    blocks(1, (0,))
    forward(0)
    blocks(0, (1, 3, 2, 0))
    for j in range(NX - 1):
        block_from(1, jnp.where(x <= j, j + 1, j))
    forward(1)
    second_step(0)
    second_step(1)
    forward(2)

    def rf(d):
        w = rem(v + d, 16)
        to = ring(w)
        return remote(s4.at[rem(div(w, 2), 2), to["group"]], r3.at[v], os_.at[2], or_.at[2], to)

    fb = remote(s3.at[0, 1 - zl], b3.at[0], os_.at[0], or_.at[0], ring(vp))
    fa = remote(s3.at[1, 1 - zl], b3.at[1], os_.at[1], or_.at[1], ring(vp))
    stays = [pltpu.make_async_copy(s3.at[u, zl], kept.at[u], lsem.at[5]) for u in range(2)]
    fill = pltpu.make_async_copy(s3.at[1, zl, 0], r3.at[v], lsem.at[6])
    third_step(1)
    _, target, leaves = out_to[1]
    for i in range(2):
        for h in range(NG):
            last = leaves & (div(target, req) == h)
            s4[i, h] = jnp.where(last, s3[1, i, 1], s3[1, i, 0])
    for d in far_z:
        rf(d).start()
    fa.start()
    fill.start()
    third_step(0)
    fb.start()
    for copy in stays:
        copy.start()
    fb.wait()
    fa.wait()
    fill.wait()
    pltpu.make_async_copy(kept, kept, lsem.at[5]).wait()
    arrived(r3.at[pl.ds(0, 15)], or_.at[2])
    for c in range(n_cuts):
        own[c].wait()
        arrived(sel[c].at[pl.ds(0, NG - 1)], p2r.at[c])

    left(rq.at[pl.ds(0, 15)], zs.at[2])
    left(r3.at[pl.ds(0, 15)], os_.at[2])
    for u in range(2):
        left(gq.at[u, x, pl.ds(0, NY - 1)], as_.at[u])
        left(gq.at[u, pl.ds(0, NX - 1)], xs.at[u])
        left(s1.at[u, pl.ds(0, NX - 1)], ms.at[u, 0])
        left(t1.at[u, pl.ds(0, NX - 1)], ms.at[u, 1])
        left(s2.at[u, pl.ds(0, NY - 1)], ns.at[u])
    for c in range(n_cuts):
        left(st[c].at[pl.ds(0, NG - 1)], p1s.at[c])
        left(sel[c].at[pl.ds(0, NG - 1)], p2s.at[c])


def finish(lens_h, moves_h, mine_h, b3_h, r3_h, moved, ob_h, lb_h, oa_h, la_h, moved_to,
           lens, moves, mine, b3, r3, ob, lb, oa, la, hold, sems):
    req = ob.shape[0]
    g, zl = lax.axis_index("group"), rem(lax.axis_index("seq"), 2)
    takes = [pltpu.make_async_copy(moved.at[r], hold.at[r], sems.at[0, r]) for r in range(req)]
    puts = [pltpu.make_async_copy(hold.at[r], moved_to.at[r], sems.at[1, r]) for r in range(req)]
    loads = [
        pltpu.make_async_copy(a, b, sems.at[0, req + i])
        for i, (a, b) in enumerate(((lens_h, lens), (moves_h, moves), (mine_h, mine), (b3_h, b3), (r3_h, r3)))
    ]
    stores = [
        pltpu.make_async_copy(a, b, sems.at[1, req + i])
        for i, (a, b) in enumerate(((ob, ob_h), (lb, lb_h), (oa, oa_h), (la, la_h)))
    ]
    for copy in takes + loads:
        copy.start()
    for copy in loads:
        copy.wait()
    table = read_table(moves)
    for r in range(req):
        alive = lens[g * req + r] > 0
        out, lse = join([mine[0, r], b3[0, r]])
        ob[r] = jnp.where(alive, out, 0.0).astype(BF16)
        lb[r : r + 1, :] = to_row(jnp.where(alive, lse, 0.0))[:, 0:2]
        _, _, leaves = look(table, lambda m, r=r: (m[0] == g) & (m[1] == r))
        stays = alive & jnp.logical_not(leaves)
        out, lse = join([mine[1, r], b3[1, r]])
        oa[r] = jnp.where(stays, out, 0.0).astype(BF16)
        la[:, r : r + 1] = jnp.where(stays, lse, 0.0)
    for copy, put in zip(takes, puts):
        copy.wait()
        put.start()
    for k in range(req):
        a, _, found = look(table, lambda m, k=k: (m[2] == g) & (m[3] == k))
        sg = div(a, req)
        out, lse = join([r3[(div(sg, 2) * 2 + i) * 2 + rem(sg, 2)] for i in range(2)])
        alive = found & (lens[a] > 0)
        oa[req + k] = jnp.where(alive, out, 0.0).astype(BF16)
        la[:, req + k : req + k + 1] = jnp.where(alive, lse, 0.0)
    for copy in stores:
        copy.start()
    for copy in stores + puts:
        copy.wait()


def local(cache, lengths, moves, qb, qa):
    req, shard, width = cache.shape
    heads = qb.shape[1]
    n = NY * 8
    wide = LAT + 128
    vm, dma = pltpu.VMEM, pltpu.SemaphoreType.DMA
    hbm = pl.BlockSpec(memory_space=pltpu.HBM)
    shape = jax.ShapeDtypeStruct
    outs = (
        shape((req, heads, LAT), BF16),
        shape((req, heads), F32),
        shape((2 * req, heads, LAT), BF16),
        shape((heads, 2 * req), F32),
        shape((req, width, shard), BF16),
    )
    sent = (
        shape((2, req, heads, wide), BF16),
        shape((2, req, heads, wide), BF16),
        shape((16, heads, wide), BF16),
        outs[4],
    )
    moves = moves.T
    got = pl.pallas_call(
        kernel,
        out_shape=sent,
        in_specs=[hbm] * 5,
        out_specs=(hbm,) * 4,
        scratch_shapes=[
            pltpu.SMEM(lengths.shape, jnp.int32),
            pltpu.SMEM(moves.shape, jnp.int32),
            pltpu.SMEM((3, NG * req), jnp.int32),
            vm(qb.shape, BF16),
            vm(qa.shape, BF16),
            vm((req, width, shard), BF16),
            *[tuple(vm((NG, req, size, 128), BF16) for size in CUTS)] * 2,
            vm((16, heads, width), BF16),
            vm((NG, heads, width), BF16),
            vm((req, heads, width), BF16),
            vm((req, heads, width), BF16),
            vm((2, 8, width), F32),
            vm((2, NX, NY, 8, width), BF16),
            vm((2, NX, n, LAT), BF16), vm((2, NX, n, LAT), BF16),
            vm((2, NX, 1, 128), F32), vm((2, NX, 1, 128), F32),
            vm((2, NY, 8, wide), BF16), vm((2, NY, 8, wide), BF16),
            vm((2, 2, req, heads, wide), BF16),
            vm((2, NG, heads, wide), BF16),
            dma((7 + 2 * len(CUTS),)),
            *[dma((len(CUTS),))] * 4,
            dma((3,)), dma((3,)),
            dma((2,)), dma((2, 3)),
            dma((2,)), dma((2, NX)),
            dma((2, 2)), dma((2, 2)),
            dma((2,)), dma((2,)),
            dma((3,)), dma((3,)),
        ],
        name="decode_and_move",
        compiler_params=pltpu.CompilerParams(
            collective_id=0, has_side_effects=True, vmem_limit_bytes=63 << 20
        ),
    )(lengths, moves, jnp.transpose(cache, (0, 2, 1)), qb, qa)
    ob, lb, oa, la, moved = pl.pallas_call(
        finish,
        out_shape=outs,
        in_specs=[hbm] * 6,
        out_specs=(hbm,) * 5,
        scratch_shapes=[
            pltpu.SMEM(lengths.shape, jnp.int32),
            pltpu.SMEM(moves.shape, jnp.int32),
            *(vm(o.shape, o.dtype) for o in sent[:3]),
            *(vm(o.shape, o.dtype) for o in outs),
            dma((2, req + 5)),
        ],
        name="finish",
        compiler_params=pltpu.CompilerParams(vmem_limit_bytes=63 << 20),
    )(lengths, moves, *got)
    return ob, lb, oa, la.T, jnp.transpose(moved, (0, 2, 1))


def solution(mesh):
    placed = (P("group", "seq", None), P(), P(), P("group", "seq", None), P("group", "seq", None))
    return jax.shard_map(
        local,
        mesh=mesh,
        in_specs=placed,
        out_specs=(
            P("group", "seq", None),
            P("group", "seq"),
            P("group", "seq", None),
            P("group", "seq"),
            P("group", "seq", None),
        ),
        check_vma=False,
    )
```
